256 devices in a mesh: rep: 4 (over z_hi), section: 4 (over z_lo, core), tp: 16 (over y, x).
Axes of the slice: x: 4, y: 4, z: 8 (z_hi: 4, z_lo: 2; z = z_hi * 2 + z_lo), core: 2. Of those that a mesh axis runs over, the one named last changes fastest.
Arguments:
- layer_section: int32 [4, 6], replicated, may hold values from 0 to 3, as said below
- token_count: int32 [4], replicated, may hold values from 1 to 1536, 3840 in all
- window_size: int32 [6], replicated, may hold values from 192 to 768, as said below
- normed_input: bfloat16 [4, 4, 2, 1536, 6144], P('rep', 'section', None, None, 'tp'), may hold values from -6 to 6
- queries: bfloat16 [4, 4, 2, 1536, 4096], P('rep', 'section', None, None, 'tp'), may hold values from -6 to 6
- key_rows: bfloat16 [4, 4, 2, 1536, 512], P('rep', 'section'), may hold values from -6 to 6
- out_grad: bfloat16 [4, 4, 2, 1536, 4096], P('rep', 'section', None, None, 'tp'), may hold values from -6 to 6
- master: float32 [6, 16, 384, 512], P(None, 'tp', ('rep', 'section')), may hold values from -6 to 6
- moment_one: float32 [6, 16, 384, 512], P(None, 'tp', ('rep', 'section')), may hold values from -12 to 12
- moment_two: float32 [6, 16, 384, 512], P(None, 'tp', ('rep', 'section')), may hold values from 1 to 20
Outputs:
- new_master: float32 [6, 16, 384, 512], P(None, 'tp', ('rep', 'section'))
- new_moment_one: float32 [6, 16, 384, 512], P(None, 'tp', ('rep', 'section'))
- new_moment_two: float32 [6, 16, 384, 512], P(None, 'tp', ('rep', 'section'))
- compute_weights: bfloat16 [4, 4, 2, 6144, 512], P('rep', 'section', None, 'tp')
The draws below stay inside these ranges and needn't reach their ends.
Inputs may be any that keep to these rules, and one draw needn't show every extreme that they name: layer_section[r, l] never falls as l grows, and every section of every replica holds 1 or 2 layers. Rows from token_count[r] on are padding; the largest count is exactly 1536. `window_size`: query i sees keys i - w + 1 to i; one layer has exactly 768 and one exactly 192.
All inputs are finite; a program needn't handle non-finite values.
Results may differ from the reference program's by a relative error of at most 0.02.
Values may be sent and summed in bfloat16 or wider, within the bound.
No kernel may reach another device: no remote copies, remote signals or barrier semaphores. Data moves between devices by JAX's collectives and lax.ppermute only.
A program may use at most 128 MiB of HBM per device.

```python
import math
import jax
import jax.numpy as jnp
import numpy as np
from jax import lax

D = 6144
HQ = 32
KVH = 4
HD = 128
SEQ_LEN = 1536
LMAX = 2
LAYERS = 6
DTP = 384
N_REP = 4
N_SECTION = 4
N_TP = 16


def draw_layer_section(key, part):
    key = jax.random.fold_in(key, 11)
    subkeys = jax.random.split(key, N_REP)

    def one_replica(subkey):
        order = jax.random.permutation(subkey, N_SECTION)
        held = 1 + (order < N_SECTION // 2).astype(jnp.int32)
        ends = jnp.cumsum(held)
        layer_ids = jnp.arange(LAYERS)
        return jnp.sum((ends[None, :] <= layer_ids[:, None]).astype(jnp.int32), axis=1)
    return jax.vmap(one_replica)(subkeys).astype(jnp.int32)


def draw_window_size(key, part):
    key = jax.random.fold_in(key, 12)
    first_key, second_key = jax.random.split(key)
    base = jax.random.randint(first_key, (LAYERS,), SEQ_LEN // 8, SEQ_LEN // 2 + 1)
    order = jax.random.permutation(second_key, LAYERS)
    base = jnp.where(order == 0, SEQ_LEN // 2, base)
    base = jnp.where(order == 1, SEQ_LEN // 8, base)
    return base.astype(jnp.int32)


def draw_queries(key, part):
    key = jax.random.fold_in(key, 21)
    shape = (N_REP, N_SECTION, LMAX, SEQ_LEN, HQ * HD)
    return jax.random.truncated_normal(key, -6.0, 6.0, shape, jnp.float32).astype(jnp.bfloat16)


def draw_key_rows(key, part):
    key = jax.random.fold_in(key, 22)
    shape = (N_REP, N_SECTION, LMAX, SEQ_LEN, KVH * HD)
    return jax.random.truncated_normal(key, -6.0, 6.0, shape, jnp.float32).astype(jnp.bfloat16)


def block_scale(key, extent, cuts, smallest, high):
    factor_of, own = 1.0, jax.random.fold_in(key, 6)
    for position, shards_of in cuts:
        draws = jnp.exp(jax.random.uniform(jax.random.fold_in(own, position), (shards_of,), jnp.float32, smallest / len(cuts), high / len(cuts)))
        factor_of = factor_of * jnp.repeat(draws, extent[position] // shards_of).reshape([-1 if axis == position else 1 for axis in range(len(extent))])
    return factor_of


def split_up(count, total, limit, lean):
    loads = [(1 << 20) // math.isqrt(rank ** lean) + 1 for rank in range(2, count + 1)]
    surplus, holding = total - limit - (count - 1), [1] * (count - 1)
    while surplus > 0:
        free = [i for i in range(count - 1) if holding[i] < limit]
        mass, remaining = sum([loads[i] for i in free]), surplus
        for i in free:
            more = min(limit - holding[i], max(1, remaining * loads[i] // mass), surplus)
            holding[i] = holding[i] + more
            surplus = surplus - more
    return np.array([limit] + holding)


def uneven_parts(rng, count, total, reach, skew):
    if count == 2:
        one = jax.random.randint(rng, (), max(1, total - reach), min(reach, total - 1) + 1)
        return jnp.stack([one, total - one])
    lengths = jnp.asarray(split_up(count, total, reach, skew), jnp.int32)
    couples = (count - 1) // 2
    source_of, receiver = lengths[1:1 + 2 * couples:2], lengths[2:2 + 2 * couples:2]
    margin = jnp.minimum(source_of - 1, reach - receiver)
    shifted = jax.random.randint(jax.random.fold_in(rng, 1), (couples,), 0, 1 << 20) % (margin + 1)
    lengths = lengths.at[1:1 + 2 * couples:2].set(source_of - shifted).at[2:2 + 2 * couples:2].set(receiver + shifted)
    return lengths[jax.random.permutation(jax.random.fold_in(rng, 2), count)]


def scatter_about(key, dims, deviation, reach, cuts=(), kind=jnp.bfloat16):
    array = jax.random.normal(key, dims, jnp.float32) * deviation
    if len(cuts) > 0:
        array = block_scale(key, dims, cuts, -0.22, 0.18) * array
    return jnp.clip(array, min=-reach, max=reach).astype(kind)


def setup_inputs(seed: int = 0) -> dict:
    seeds = jax.random.split(jax.random.key(seed), 11)
    return {
        "layer_section": draw_layer_section(jax.random.fold_in(seeds[10], 71), 0),
        "token_count": uneven_parts(seeds[1], N_REP, SEQ_LEN + (N_REP - 1) * SEQ_LEN // 2, SEQ_LEN, 1).astype(jnp.int32),
        "window_size": draw_window_size(jax.random.fold_in(seeds[10], 71), 0),
        "normed_input": scatter_about(seeds[3], (N_REP, N_SECTION, LMAX, SEQ_LEN, D), 1.0, 6.0, ((0, 4), (1, 4), (4, 16))),
        "queries": draw_queries(jax.random.fold_in(seeds[10], 71), 0),
        "key_rows": draw_key_rows(jax.random.fold_in(seeds[10], 71), 0),
        "out_grad": scatter_about(seeds[6], (N_REP, N_SECTION, LMAX, SEQ_LEN, HQ * HD), 1.0, 6.0, ((0, 4), (1, 4), (4, 16))),
        "master": scatter_about(seeds[7], (LAYERS, N_TP, DTP, KVH * HD), 1.0, 6.0, ((1, 16), (2, 16)), jnp.float32),
        "moment_one": scatter_about(seeds[8], (LAYERS, N_TP, DTP, KVH * HD), 2.0, 12.0, ((1, 16), (2, 16)), jnp.float32),
        "moment_two": jnp.clip(jnp.exp(math.log(20.0) - 2.9957323 * jax.random.uniform(seeds[9], (LAYERS, N_TP, DTP, KVH * HD), jnp.float32) ** block_scale(seeds[9], (LAYERS, N_TP, DTP, KVH * HD), ((1, 16), (2, 16)), -0.2, 0.2)), 1.0, 20.0),
    }


BETA_ONE = 0.9
BETA_TWO = 0.95
LEARN_RATE = 0.03
DECAY_RATE = 0.1
EPSILON = 1e-08
CORRECT_ONE = 0.9999734386011124
CORRECT_TWO = 0.994079470779667

def probabilities(scores, first_row, block_rows, key_span, reach_back, length, window):
    row_ids = first_row + jnp.arange(block_rows)
    key_ids = first_row - reach_back + jnp.arange(key_span)
    allowed = (key_ids[None, :] <= row_ids[:, None]) & (key_ids[None, :] > row_ids[:, None] - window) & (key_ids[None, :] >= 0)
    masked = jnp.where(allowed[None], scores, -1e+30)
    peak_score = lax.optimization_barrier(jnp.max(masked, axis=-1, keepdims=True))
    raised = jnp.exp(masked - peak_score)
    normed = raised / lax.optimization_barrier(jnp.sum(raised, axis=-1, keepdims=True))
    normed = jnp.where((row_ids < length)[None, :, None], normed, 0.0)
    return normed.astype(jnp.bfloat16)

def head_terms(query_rows, keyset, grad_rows, length, window):
    tokens = query_rows.shape[0]
    block_rows = min(512, tokens)
    reach_back = tokens // 2
    key_span = block_rows + reach_back
    kv_index = jnp.arange(HQ) // (HQ // KVH)
    keys_head = jnp.take(keyset.reshape(tokens, KVH, HD), kv_index, axis=1).astype(jnp.float32)
    keys_head = jnp.pad(keys_head, ((reach_back, 0), (0, 0), (0, 0)))
    query_head = query_rows.reshape(tokens, HQ, HD).astype(jnp.float32)
    grad_head = grad_rows.reshape(tokens, HQ, HD).astype(jnp.float32)
    accumulated = jnp.zeros((reach_back + tokens, HQ, HD), jnp.float32)
    for block_index in range(tokens // block_rows):
        first_row = block_index * block_rows
        scores = jnp.einsum('qhd,khd->hqk', query_head[first_row:first_row + block_rows], keys_head[first_row:first_row + key_span]) * HD ** (-0.5)
        weights_bf = probabilities(scores, first_row, block_rows, key_span, reach_back, length, window)
        head_term = jnp.einsum('hqk,qhd->khd', weights_bf.astype(jnp.float32), grad_head[first_row:first_row + block_rows])
        accumulated = accumulated.at[first_row:first_row + key_span].add(head_term)
    return accumulated[reach_back:]

def reference(layer_section, token_count, window_size, normed_input, queries, key_rows, out_grad, master, moment_one, moment_two):
    per_dev = HQ // N_TP
    kv_index = (jnp.arange(HQ) // (HQ // KVH)).reshape(N_TP, per_dev)
    select = (kv_index[:, :, None] == jnp.arange(KVH)[None, None, :]).astype(jnp.float32)
    layer_grads = []
    for layer_id in range(LAYERS):
        summed = jnp.zeros((D, KVH * HD), jnp.float32)
        for replica in range(N_REP):
            section_id = layer_section[replica, layer_id]
            first_layer = jnp.sum((layer_section[replica] < section_id).astype(jnp.int32))
            slot_id = (layer_id - first_layer).astype(jnp.int32)
            terms = head_terms(queries[replica, section_id, slot_id], key_rows[replica, section_id, slot_id], out_grad[replica, section_id, slot_id], token_count[replica], window_size[layer_id])
            device_terms = terms.reshape(SEQ_LEN, N_TP, per_dev, HD)
            partial_value = jnp.einsum('tnhd,nhk->ntkd', device_terms, select, precision=lax.Precision.HIGHEST)
            rounded = lax.optimization_barrier(partial_value.astype(jnp.bfloat16)).astype(jnp.float32)
            value_grad = lax.optimization_barrier(jnp.sum(rounded, axis=0)).reshape(SEQ_LEN, KVH * HD).astype(jnp.bfloat16)
            summed = summed + jnp.dot(normed_input[replica, section_id, slot_id].T, value_grad, preferred_element_type=jnp.float32)
        layer_grads.append(summed / N_REP)
    mean_grad = jnp.stack(layer_grads).reshape(LAYERS, N_TP, D // N_TP, KVH * HD)
    first = BETA_ONE * moment_one + (1.0 - BETA_ONE) * mean_grad
    second = BETA_TWO * moment_two + (1.0 - BETA_TWO) * mean_grad * mean_grad
    adam_step = first / CORRECT_ONE / (jnp.sqrt(second / CORRECT_TWO) + EPSILON)
    updated = master - LEARN_RATE * (adam_step + DECAY_RATE * master)
    flat_rows = updated.reshape(LAYERS, D, KVH * HD).astype(jnp.bfloat16)
    blocks = []
    for replica in range(N_REP):
        for section_id in range(N_SECTION):
            first_layer = jnp.sum((layer_section[replica] < section_id).astype(jnp.int32))
            held_count = jnp.sum((layer_section[replica] == section_id).astype(jnp.int32))
            for slot_id in range(LMAX):
                layer_of = jnp.clip(first_layer + slot_id, 0, LAYERS - 1).astype(jnp.int32)
                blocks.append(jnp.where(slot_id < held_count, flat_rows[layer_of], jnp.zeros_like(flat_rows[0])))
    compute_weights = jnp.stack(blocks).reshape(N_REP, N_SECTION, LMAX, D, KVH * HD)
    return (updated, first, second, compute_weights)
```

```python
import functools

import jax
import jax.numpy as jnp
from jax import lax
from jax.experimental import pallas as pl
from jax.experimental.pallas import tpu as pltpu
from jax.sharding import Mesh, PartitionSpec as P

HQ = 32
KVH = 4
HD = 128
BETA_ONE = 0.9
BETA_TWO = 0.95
LEARN_RATE = 0.03
DECAY_RATE = 0.1
EPSILON = 1e-08
CORRECT_ONE = 0.9999734386011124
CORRECT_TWO = 0.994079470779667
LOG2E = 1.4426950408889634
TQ = 256
SECTIONS = 4
BF = jnp.bfloat16
F32 = jnp.float32


def first_and_count(map_ref, replica, section, layers):
    first = jnp.int32(0)
    count = jnp.int32(0)
    for l in range(layers):
        at = map_ref[replica, l]
        first += (at < section).astype(jnp.int32)
        count += (at == section).astype(jnp.int32)
    return first, count


def attention_kernel(slot, layers, tokens, per_dev, ids, lmap, counts, windows,
                     q_ref, k_ref, g_ref, *rest):
    outs = rest[:4]
    acc, p_scr, g_scr = rest[4:]
    step = pl.program_id(0)
    steps = pl.num_programs(0)
    replica, section, x_id = ids[0], ids[1], ids[3]
    first, held = first_and_count(lmap, replica, section, layers)
    layer = jnp.minimum(first + slot, layers - 1)
    window = windows[layer]
    length = jnp.where(slot < held, counts[replica], 0)
    reach = tokens // 2 // TQ
    row0 = step * TQ

    @pl.when(step == 0)
    def _():
        acc[...] = jnp.zeros_like(acc)

    def work(chunks):
        base = pl.multiple_of((step - (chunks - 1)) * TQ, TQ)
        keys = k_ref[pl.ds(base, chunks * TQ), :]
        q_col = lax.broadcasted_iota(jnp.int32, (TQ, TQ), 1)
        k_row = lax.broadcasted_iota(jnp.int32, (TQ, TQ), 0)
        diff = q_col - k_row
        live = (row0 + lax.broadcasted_iota(jnp.int32, (TQ, HD), 0)) < length
        scale = HD ** (-0.5) * LOG2E
        for h in range(per_dev):
            query = q_ref[:, h * HD:(h + 1) * HD]
            parts = []
            peak = None
            for c in range(chunks):
                s = lax.dot_general(
                    keys[c * TQ:(c + 1) * TQ], query, (((1,), (1,)), ((), ())),
                    preferred_element_type=F32)
                off = (chunks - 1 - c) * TQ
                ok = diff < (window - off)
                if c == chunks - 1:
                    ok = ok & (diff >= 0)
                s = jnp.where(ok, s, -1e30)
                parts.append(s)
                m = jnp.max(s, axis=0, keepdims=True)
                peak = m if peak is None else jnp.maximum(peak, m)
            shift = peak * scale
            total = None
            for c in range(chunks):
                e = jnp.exp2(parts[c] * scale - shift)
                t = jnp.sum(e, axis=0, keepdims=True)
                total = t if total is None else total + t
                p_scr[c * TQ:(c + 1) * TQ, h * TQ:(h + 1) * TQ] = e.astype(BF)
            inverse = jnp.broadcast_to(1.0 / total, (HD, TQ)).T
            grad = g_ref[:, h * HD:(h + 1) * HD].astype(F32) * inverse
            g_scr[h * TQ:(h + 1) * TQ, :] = jnp.where(live, grad, 0.0).astype(BF)
        for c in range(chunks):
            rows = pl.ds(base + c * TQ, TQ)
            acc[rows, :] += jnp.dot(
                p_scr[c * TQ:(c + 1) * TQ, :], g_scr[...], preferred_element_type=F32)

    wanted = jnp.minimum(step, (window + TQ - 2) // TQ) + 1
    for chunks in range(1, reach + 2):
        @pl.when((row0 < length) & (wanted == chunks))
        def _(chunks=chunks):
            work(chunks)

    @pl.when(step == steps - 1)
    def _():
        part = tokens // 4
        for k in range(4):
            at = pl.multiple_of(lax.rem(x_id + k, 4) * part, part)
            outs[k][...] = acc[pl.ds(at, part), :].astype(BF)


def attention(slot, scalars, queries, key_rows, out_grad, layers):
    tokens = queries.shape[3]
    per_dev = queries.shape[4] // HD
    steps = tokens // TQ
    part = tokens // 4
    wide = per_dev * HD
    row_block = pl.BlockSpec((None, None, None, TQ, wide), lambda i, *_: (0, 0, slot, i, 0))
    key_block = pl.BlockSpec(
        (None, None, None, tokens, HD), lambda i, ids, *_: (0, 0, slot, 0, ids[2]))
    out_block = pl.BlockSpec((part, HD), lambda i, *_: (0, 0))
    return pl.pallas_call(
        functools.partial(attention_kernel, slot, layers, tokens, per_dev),
        grid_spec=pltpu.PrefetchScalarGridSpec(
            num_scalar_prefetch=4,
            grid=(steps,),
            in_specs=[row_block, key_block, row_block],
            out_specs=[out_block] * 4,
            scratch_shapes=[
                pltpu.VMEM((tokens, HD), F32),
                pltpu.VMEM((tokens // 2 + TQ, per_dev * TQ), BF),
                pltpu.VMEM((per_dev * TQ, HD), BF),
            ],
        ),
        out_shape=[jax.ShapeDtypeStruct((part, HD), BF)] * 4,
        compiler_params=pltpu.CompilerParams(vmem_limit_bytes=40 << 20),
        cost_estimate=pl.CostEstimate(
            flops=18 * per_dev * 4 * TQ * TQ * HD, bytes_accessed=2 << 20,
            transcendentals=18 * per_dev * TQ * TQ),
        name="attn%d" % slot,
    )(*scalars, queries, key_rows, out_grad)


def grad_kernel(tokens, ids, x_ref, *refs):
    own_p, px, own_q, qy, py, qx = refs[0], refs[1:4], refs[4], refs[5:8], refs[8:11], refs[11:14]
    out_ref, value = refs[14], refs[15]
    y_id, x_id = ids[2], ids[3]
    part = tokens // 4
    half = part // 2

    def put(block, y, x, second):
        y = lax.rem(y_id + 4 - y, 4)
        x = lax.rem(x_id + 4 - x, 4)
        at = pl.multiple_of(x * part + second * half, half)
        col = pl.multiple_of(y * HD, HD)
        value[pl.ds(at, half), pl.ds(col, HD)] = block

    put(own_p[...], 0, 0, 0)
    put(own_q[...], 0, 0, 1)
    for k in range(1, 4):
        put(px[k - 1][...], 0, k, 0)
        put(qy[k - 1][...], k, 0, 1)
        for i in range(4):
            put(py[k - 1][i], k, i, 0)
            put(qx[k - 1][i], i, k, 1)
    out_ref[...] = lax.dot_general(
        x_ref[...], value[...], (((0,), (0,)), ((), ())),
        preferred_element_type=F32).astype(BF)


def layer_grad(slot, scalars, normed, pieces):
    tokens, width = normed.shape[3], normed.shape[4]
    whole = pl.BlockSpec(memory_space=pltpu.VMEM)
    return pl.pallas_call(
        functools.partial(grad_kernel, tokens),
        grid_spec=pltpu.PrefetchScalarGridSpec(
            num_scalar_prefetch=1,
            grid=(1,),
            in_specs=[pl.BlockSpec((None, None, None, tokens, width),
                                   lambda i, *_: (0, 0, slot, 0, 0))] + [
                pl.BlockSpec(p.shape, lambda i, *_, n=p.ndim: (0,) * n) for p in pieces],
            out_specs=pl.BlockSpec((width, KVH * HD), lambda i, *_: (0, 0)),
            scratch_shapes=[pltpu.VMEM((tokens, KVH * HD), BF)],
        ),
        out_shape=jax.ShapeDtypeStruct((width, KVH * HD), BF),
        compiler_params=pltpu.CompilerParams(vmem_limit_bytes=40 << 20),
        cost_estimate=pl.CostEstimate(
            flops=2 * tokens * width * KVH * HD, bytes_accessed=3 << 20, transcendentals=0),
        name="grad%d" % slot,
    )(scalars[0], normed, *pieces)


def adam_kernel(reps, layers, lmap, first_ref, second_ref, master, one, two,
                new_master, new_one, new_two, send):
    layer = pl.program_id(0)

    @pl.when(layer == 0)
    def _():
        send[...] = jnp.zeros_like(send)

    total = None
    places = []
    for r in range(reps):
        section = lmap[r, layer]
        first, _ = first_and_count(lmap, r, section, layers)
        slot = layer - first
        source = r * SECTIONS + section
        places.append((source, slot))
        term = jnp.where(slot == 0, first_ref[source].astype(F32), second_ref[source].astype(F32))
        total = term if total is None else total + term
    mean = total / reps
    m1 = BETA_ONE * one[...] + (1.0 - BETA_ONE) * mean
    m2 = BETA_TWO * two[...] + (1.0 - BETA_TWO) * mean * mean
    move = m1 / CORRECT_ONE / (jnp.sqrt(m2 / CORRECT_TWO) + EPSILON)
    updated = master[...] - LEARN_RATE * (move + DECAY_RATE * master[...])
    new_master[...] = updated
    new_one[...] = m1
    new_two[...] = m2
    rounded = updated.astype(BF)
    for source, slot in places:
        send[source, slot] = rounded


def adam(lmap, received, master, one, two):
    layers, _, rows, wide = master.shape
    group = received[0].shape[0]
    slots = 2
    state = pl.BlockSpec((None, None, rows, wide), lambda l, *_: (l, 0, 0, 0))
    whole = pl.BlockSpec((group, rows, wide), lambda l, *_: (0, 0, 0))
    f32 = jax.ShapeDtypeStruct(master.shape, F32)
    return pl.pallas_call(
        functools.partial(adam_kernel, lmap.shape[0], layers),
        grid_spec=pltpu.PrefetchScalarGridSpec(
            num_scalar_prefetch=1,
            grid=(layers,),
            in_specs=[whole, whole, state, state, state],
            out_specs=[state, state, state,
                       pl.BlockSpec((group, slots, rows, wide), lambda l, *_: (0, 0, 0, 0))],
        ),
        out_shape=[f32, f32, f32, jax.ShapeDtypeStruct((group, slots, rows, wide), BF)],
        compiler_params=pltpu.CompilerParams(vmem_limit_bytes=40 << 20),
        cost_estimate=pl.CostEstimate(flops=20 * master.size, bytes_accessed=4 << 20,
                                      transcendentals=master.size),
        name="adamw",
    )(lmap, *received, master, one, two)


def shift(value, axis, by):
    n = lax.axis_size(axis)
    return lax.ppermute(value, axis, [(i, (i + by) % n) for i in range(n)])


def gather_pieces(block):
    half = block.shape[0] // 2
    p, q = block[:half], block[half:]
    px = [shift(p, "x", k) for k in range(1, 4)]
    qy = [shift(q, "y", k) for k in range(1, 4)]
    p_row = jnp.stack([p] + px)
    q_col = jnp.stack([q] + qy)
    py = [shift(p_row, "y", k) for k in range(1, 4)]
    qx = [shift(q_col, "x", k) for k in range(1, 4)]
    return [p] + px + [q] + qy + py + qx


def body(layer_section, token_count, window_size, normed_input, queries, key_rows, out_grad,
         master, moment_one, moment_two):
    layers = layer_section.shape[1]
    group_axes = ("rep", "z", "core")
    ids = jnp.stack([
        lax.axis_index("rep"), lax.axis_index(("z", "core")),
        lax.axis_index("y"), lax.axis_index("x")]).astype(jnp.int32)
    scalars = (ids, layer_section, token_count, window_size)
    rows = master.shape[2]
    received = []
    for slot in range(2):
        parts = attention(slot, scalars, queries, key_rows, out_grad, layers)
        total = parts[0].astype(F32)
        for k in range(1, 4):
            total = total + shift(parts[k], "x", k).astype(F32)
        pieces = gather_pieces(total.astype(BF))
        grad = layer_grad(slot, scalars, normed_input, pieces)
        grad = grad.reshape(-1, rows, grad.shape[1])
        received.append(lax.all_to_all(grad, group_axes, 0, 0, tiled=True))
    updated, first, second, send = adam(layer_section, received, master, moment_one, moment_two)
    arrived = lax.all_to_all(send, group_axes, 0, 0, tiled=True)
    own = jnp.transpose(arrived, (1, 0, 2, 3)).reshape(2, -1, arrived.shape[3])
    return updated, first, second, own[None, None]


def solution(mesh):
    reps, sections, tps = mesh.devices.shape
    fine = Mesh(mesh.devices.reshape(reps, 2, sections // 2, 4, tps // 4),
                ("rep", "z", "core", "y", "x"))
    section, tp = ("z", "core"), ("y", "x")
    wide = P("rep", section, None, None, tp)
    state = P(None, tp, ("rep",) + section, None)
    in_specs = (P(), P(), P(), wide, wide, P("rep", section, None, None, None), wide,
                state, state, state)
    out_specs = (state, state, state, P("rep", section, None, tp, None))
    return jax.shard_map(body, mesh=fine, in_specs=in_specs, out_specs=out_specs, check_vma=False)
```

```python
import functools

import jax
import jax.numpy as jnp
from jax import lax
from jax.experimental import pallas as pl
from jax.experimental.pallas import tpu as pltpu
from jax.sharding import Mesh, PartitionSpec as P

HQ = 32
KVH = 4
HD = 128
BETA_ONE = 0.9
BETA_TWO = 0.95
LEARN_RATE = 0.03
DECAY_RATE = 0.1
EPSILON = 1e-08
CORRECT_ONE = 0.9999734386011124
CORRECT_TWO = 0.994079470779667
LOG2E = 1.4426950408889634
TQ = 256
VMEM = 60 << 20
BF = jnp.bfloat16
F32 = jnp.float32


def first_and_count(map_ref, replica, section, layers):
    first = jnp.int32(0)
    count = jnp.int32(0)
    for l in range(layers):
        at = map_ref[replica, l]
        first += (at < section).astype(jnp.int32)
        count += (at == section).astype(jnp.int32)
    return first, count


def attention_kernel(layers, tokens, per_dev, ids, lmap, counts, windows,
                     q_ref, k_ref, g_ref, *rest):
    outs = rest[:4]
    acc, p_scr, g_scr = rest[4:]
    slot, step = pl.program_id(0), pl.program_id(1)
    steps = pl.num_programs(1)
    replica, section, x_id = ids[0], ids[1], ids[3]
    first, held = first_and_count(lmap, replica, section, layers)
    layer = jnp.minimum(first + slot, layers - 1)
    window = windows[layer]
    length = jnp.where(slot < held, counts[replica], 0)
    reach = tokens // 2 // TQ
    row0 = step * TQ

    @pl.when(step == 0)
    def _():
        acc[...] = jnp.zeros_like(acc)

    def work(chunks):
        base = pl.multiple_of((step - (chunks - 1)) * TQ, TQ)
        keys = k_ref[pl.ds(base, chunks * TQ), :]
        q_col = lax.broadcasted_iota(jnp.int32, (TQ, TQ), 1)
        k_row = lax.broadcasted_iota(jnp.int32, (TQ, TQ), 0)
        diff = q_col - k_row
        live = (row0 + lax.broadcasted_iota(jnp.int32, (TQ, HD), 0)) < length
        scale = HD ** (-0.5) * LOG2E
        for h in range(per_dev):
            query = q_ref[:, h * HD:(h + 1) * HD]
            parts = []
            peak = None
            for c in range(chunks):
                s = lax.dot_general(
                    keys[c * TQ:(c + 1) * TQ], query, (((1,), (1,)), ((), ())),
                    preferred_element_type=F32)
                off = (chunks - 1 - c) * TQ
                ok = diff < (window - off)
                if c == chunks - 1:
                    ok = ok & (diff >= 0)
                s = jnp.where(ok, s, -1e30)
                parts.append(s)
                m = jnp.max(s, axis=0, keepdims=True)
                peak = m if peak is None else jnp.maximum(peak, m)
            shift = peak * scale
            total = None
            for c in range(chunks):
                e = jnp.exp2(parts[c] * scale - shift)
                t = jnp.sum(e, axis=0, keepdims=True)
                total = t if total is None else total + t
                p_scr[c * TQ:(c + 1) * TQ, h * TQ:(h + 1) * TQ] = e.astype(BF)
            inverse = jnp.broadcast_to(1.0 / total, (HD, TQ)).T
            grad = g_ref[:, h * HD:(h + 1) * HD].astype(F32) * inverse
            g_scr[h * TQ:(h + 1) * TQ, :] = jnp.where(live, grad, 0.0).astype(BF)
        for c in range(chunks):
            rows = pl.ds(base + c * TQ, TQ)
            acc[rows, :] += jnp.dot(
                p_scr[c * TQ:(c + 1) * TQ, :], g_scr[...], preferred_element_type=F32)

    wanted = jnp.minimum(step, (window + TQ - 2) // TQ) + 1
    for chunks in range(1, reach + 2):
        @pl.when((row0 < length) & (wanted == chunks))
        def _(chunks=chunks):
            work(chunks)

    @pl.when(step == steps - 1)
    def _():
        part = tokens // 4
        for k in range(4):
            at = pl.multiple_of(lax.rem(x_id + k, 4) * part, part)
            outs[k][...] = acc[pl.ds(at, part), :].astype(BF)


def attention(scalars, queries, key_rows, out_grad, layers):
    slots, tokens = queries.shape[2], queries.shape[3]
    per_dev = queries.shape[4] // HD
    part = tokens // 4
    wide = per_dev * HD
    row_block = pl.BlockSpec((None, None, None, TQ, wide), lambda j, i, *_: (0, 0, j, i, 0))
    key_block = pl.BlockSpec(
        (None, None, None, tokens, HD), lambda j, i, ids, *_: (0, 0, j, 0, ids[2]))
    out_block = pl.BlockSpec((None, part, HD), lambda j, i, *_: (j, 0, 0))
    return pl.pallas_call(
        functools.partial(attention_kernel, layers, tokens, per_dev),
        grid_spec=pltpu.PrefetchScalarGridSpec(
            num_scalar_prefetch=4,
            grid=(slots, tokens // TQ),
            in_specs=[row_block, key_block, row_block],
            out_specs=[out_block] * 4,
            scratch_shapes=[
                pltpu.VMEM((tokens, HD), F32),
                pltpu.VMEM((tokens // 2 + TQ, per_dev * TQ), BF),
                pltpu.VMEM((per_dev * TQ, HD), BF),
            ],
        ),
        out_shape=[jax.ShapeDtypeStruct((slots, part, HD), BF)] * 4,
        compiler_params=pltpu.CompilerParams(vmem_limit_bytes=VMEM),
        cost_estimate=pl.CostEstimate(
            flops=36 * per_dev * 4 * TQ * TQ * HD, bytes_accessed=4 << 20,
            transcendentals=36 * per_dev * TQ * TQ),
        name="attention",
    )(*scalars, queries, key_rows, out_grad)


def grad_kernel(tokens, rows, ids, x_ref, piece_ref, own_ref, other_ref, value, result):
    core = lax.rem(ids[1], 2)
    part = tokens // 4
    for y in range(4):
        for x in range(4):
            value[x * part:(x + 1) * part, y * HD:(y + 1) * HD] = piece_ref[y * 4 + x]
    result[...] = lax.dot_general(
        x_ref[...], value[...], (((0,), (0,)), ((), ())), preferred_element_type=F32)
    for z in range(own_ref.shape[0]):
        for rel, ref in ((0, own_ref), (1, other_ref)):
            at = pl.multiple_of((2 * z + lax.rem(core + rel, 2)) * rows, 8)
            ref[z] = result[pl.ds(at, rows), :].astype(BF)


def layer_grads(ids, normed, pieces, rows):
    slots, tokens, width = normed.shape[2:]
    chips = width // rows // 2
    part = tokens // 4
    out_block = pl.BlockSpec((chips, None, rows, KVH * HD), lambda j, *_: (0, j, 0, 0))
    return pl.pallas_call(
        functools.partial(grad_kernel, tokens, rows),
        grid_spec=pltpu.PrefetchScalarGridSpec(
            num_scalar_prefetch=1,
            grid=(slots,),
            in_specs=[pl.BlockSpec((None, None, None, tokens, width),
                                   lambda j, *_: (0, 0, j, 0, 0)),
                      pl.BlockSpec((16, None, part, HD), lambda j, *_: (0, j, 0, 0))],
            out_specs=[out_block, out_block],
            scratch_shapes=[pltpu.VMEM((tokens, KVH * HD), BF),
                            pltpu.VMEM((width, KVH * HD), F32)],
        ),
        out_shape=[jax.ShapeDtypeStruct((chips, slots, rows, KVH * HD), BF)] * 2,
        compiler_params=pltpu.CompilerParams(vmem_limit_bytes=VMEM),
        cost_estimate=pl.CostEstimate(
            flops=4 * tokens * width * KVH * HD, bytes_accessed=6 << 20, transcendentals=0),
        name="layer_grads",
    )(ids, normed, pieces)


def adam_kernel(reps, layers, ids, lmap, arrived, master, one, two,
                new_master, new_one, new_two, own, other):
    layer = pl.program_id(0)
    core = lax.rem(ids[1], 2)

    @pl.when(layer == 0)
    def _():
        own[...] = jnp.zeros_like(own)
        other[...] = jnp.zeros_like(other)

    total = None
    places = []
    for r in range(reps):
        section = lmap[r, layer]
        first, _ = first_and_count(lmap, r, section, layers)
        slot = layer - first
        chip = 2 * r + section // 2
        rel = lax.rem(section + core, 2)
        places.append((rel, chip, slot))
        term = arrived[chip, rel, slot].astype(F32)
        total = term if total is None else total + term
    mean = total / reps
    m1 = BETA_ONE * one[...] + (1.0 - BETA_ONE) * mean
    m2 = BETA_TWO * two[...] + (1.0 - BETA_TWO) * mean * mean
    move = m1 / CORRECT_ONE / (jnp.sqrt(m2 / CORRECT_TWO) + EPSILON)
    updated = master[...] - LEARN_RATE * (move + DECAY_RATE * master[...])
    new_master[...] = updated
    new_one[...] = m1
    new_two[...] = m2
    rounded = updated.astype(BF)
    for rel, chip, slot in places:
        @pl.when(rel == 0)
        def _(chip=chip, slot=slot):
            own[chip, slot] = rounded

        @pl.when(rel != 0)
        def _(chip=chip, slot=slot):
            other[chip, slot] = rounded


def adam(ids, lmap, arrived, master, one, two):
    layers, _, rows, wide = master.shape
    chips, _, slots = arrived.shape[:3]
    state = pl.BlockSpec((None, None, rows, wide), lambda l, *_: (l, 0, 0, 0))
    send = pl.BlockSpec((chips, slots, rows, wide), lambda l, *_: (0, 0, 0, 0))
    f32 = jax.ShapeDtypeStruct(master.shape, F32)
    return pl.pallas_call(
        functools.partial(adam_kernel, lmap.shape[0], layers),
        grid_spec=pltpu.PrefetchScalarGridSpec(
            num_scalar_prefetch=2,
            grid=(layers,),
            in_specs=[pl.BlockSpec(arrived.shape, lambda l, *_: (0, 0, 0, 0, 0)),
                      state, state, state],
            out_specs=[state, state, state, send, send],
        ),
        out_shape=[f32, f32, f32] + [jax.ShapeDtypeStruct((chips, slots, rows, wide), BF)] * 2,
        compiler_params=pltpu.CompilerParams(vmem_limit_bytes=VMEM),
        cost_estimate=pl.CostEstimate(flops=20 * master.size, bytes_accessed=4 << 20,
                                      transcendentals=master.size),
        name="adamw",
    )(ids, lmap, arrived, master, one, two)


def shift(value, axis, by):
    n = lax.axis_size(axis)
    return lax.ppermute(value, axis, [(i, (i + by) % n) for i in range(n)])


def body(layer_section, token_count, window_size, normed_input, queries, key_rows, out_grad,
         master, moment_one, moment_two):
    layers = layer_section.shape[1]
    chip_axes = ("rep", "z")
    core = lax.axis_index("core")
    ids = jnp.stack([
        lax.axis_index("rep"), lax.axis_index(("z", "core")),
        lax.axis_index("y"), lax.axis_index("x")]).astype(jnp.int32)
    rows = master.shape[2]
    parts = attention((ids, layer_section, token_count, window_size),
                      queries, key_rows, out_grad, layers)
    total = parts[0].astype(F32)
    for k in range(1, 4):
        total = total + shift(parts[k], "x", k).astype(F32)
    block = total.astype(BF)
    spread = lax.optimization_barrier(jnp.broadcast_to(block[None], (16,) + block.shape))
    pieces = lax.all_to_all(spread, ("y", "x"), 0, 0, tiled=True)
    own, other = layer_grads(ids, normed_input, pieces, rows)
    arrived = lax.all_to_all(jnp.stack([own, shift(other, "core", 1)], axis=1),
                             chip_axes, 0, 0, tiled=True)
    updated, first, second, own, other = adam(
        ids, layer_section, arrived, master, moment_one, moment_two)
    arrived = lax.all_to_all(jnp.stack([own, shift(other, "core", 1)], axis=1),
                             chip_axes, 0, 0, tiled=True)
    arrived = jnp.where(core == 0, arrived, arrived[:, ::-1])
    weights = jnp.transpose(arrived, (2, 0, 1, 3, 4)).reshape(
        arrived.shape[2], -1, arrived.shape[4])
    return updated, first, second, weights[None, None]


def solution(mesh):
    reps, sections, tps = mesh.devices.shape
    fine = Mesh(mesh.devices.reshape(reps, 2, sections // 2, 4, tps // 4),
                ("rep", "z", "core", "y", "x"))
    section, tp = ("z", "core"), ("y", "x")
    wide = P("rep", section, None, None, tp)
    state = P(None, tp, ("rep",) + section, None)
    in_specs = (P(), P(), P(), wide, wide, P("rep", section, None, None, None), wide,
                state, state, state)
    out_specs = (state, state, state, P("rep", section, None, tp, None))
    return jax.shard_map(body, mesh=fine, in_specs=in_specs, out_specs=out_specs, check_vma=False)
```

```python
import functools

import jax
import jax.numpy as jnp
from jax import lax
from jax.experimental import pallas as pl
from jax.experimental.pallas import tpu as pltpu
from jax.sharding import Mesh, PartitionSpec as P

HQ = 32
KVH = 4
HD = 128
BETA_ONE = 0.9
BETA_TWO = 0.95
LEARN_RATE = 0.03
DECAY_RATE = 0.1
EPSILON = 1e-08
CORRECT_ONE = 0.9999734386011124
CORRECT_TWO = 0.994079470779667
LOG2E = 1.4426950408889634
TQ = 256
RB = 512
VMEM = 60 << 20
BF = jnp.bfloat16
F32 = jnp.float32


def first_and_count(map_ref, replica, section, layers):
    first = jnp.int32(0)
    count = jnp.int32(0)
    for l in range(layers):
        at = map_ref[replica, l]
        first += (at < section).astype(jnp.int32)
        count += (at == section).astype(jnp.int32)
    return first, count


def attention_kernel(layers, tokens, per_dev, ids, lmap, counts, windows,
                     q_ref, k_ref, g_ref, *rest):
    outs = rest[:4]
    acc, p_scr, g_scr = rest[4:]
    slot, step = pl.program_id(0), pl.program_id(1)
    steps = pl.num_programs(1)
    replica, section, x_id = ids[0], ids[1], ids[3]
    first, held = first_and_count(lmap, replica, section, layers)
    layer = jnp.minimum(first + slot, layers - 1)
    window = windows[layer]
    length = jnp.where(slot < held, counts[replica], 0)
    reach = tokens // 2 // TQ
    scale = HD ** (-0.5) * LOG2E

    @pl.when(step == 0)
    def _():
        acc[...] = jnp.zeros_like(acc)

    diff = (lax.broadcasted_iota(jnp.int32, (TQ, TQ), 1)
            - lax.broadcasted_iota(jnp.int32, (TQ, TQ), 0))

    def scores(sub, index, chunks, h):
        base = pl.multiple_of((index - (chunks - 1)) * TQ, TQ)
        query = q_ref[sub * TQ:(sub + 1) * TQ, h * HD:(h + 1) * HD]
        parts = []
        peak = None
        for c in range(chunks):
            s = lax.dot_general(
                k_ref[pl.ds(base + c * TQ, TQ), :], query, (((1,), (1,)), ((), ())),
                preferred_element_type=F32)
            off = (chunks - 1 - c) * TQ
            ok = None
            if c < 2:
                ok = diff < (window - off)
            if c == chunks - 1:
                ok = diff >= 0 if ok is None else ok & (diff >= 0)
            if ok is not None:
                s = jnp.where(ok, s, -1e30)
            parts.append(s)
            m = jnp.max(s, axis=0, keepdims=True)
            peak = m if peak is None else jnp.maximum(peak, m)
        return parts, peak

    def weigh(sub, index, h, parts, peak):
        shift = peak * scale
        total = None
        for c, s in enumerate(parts):
            e = jnp.exp2(s * scale - shift)
            t = jnp.sum(e, axis=0, keepdims=True)
            total = t if total is None else total + t
            p_scr[sub, c * TQ:(c + 1) * TQ, h * TQ:(h + 1) * TQ] = e.astype(BF)
        live = (index * TQ + lax.broadcasted_iota(jnp.int32, (1, TQ), 1)) < length
        inverse = jnp.where(live, 1.0 / total, 0.0)
        column = jnp.broadcast_to(inverse, (HD, TQ)).T
        grad = g_ref[sub * TQ:(sub + 1) * TQ, h * HD:(h + 1) * HD].astype(F32) * column
        g_scr[sub, h * TQ:(h + 1) * TQ, :] = grad.astype(BF)

    def spread(sub, index, chunks):
        base = pl.multiple_of((index - (chunks - 1)) * TQ, TQ)
        for c in range(chunks):
            acc[pl.ds(base + c * TQ, TQ), :] += jnp.dot(
                p_scr[sub, c * TQ:(c + 1) * TQ, :], g_scr[sub], preferred_element_type=F32)

    def pair(one, two):
        a, b = 2 * step, 2 * step + 1
        a0 = scores(0, a, one, 0)
        a1 = scores(0, a, one, 1)
        weigh(0, a, 0, *a0)
        b0 = scores(1, b, two, 0)
        weigh(0, a, 1, *a1)
        b1 = scores(1, b, two, 1)
        spread(0, a, one)
        weigh(1, b, 0, *b0)
        weigh(1, b, 1, *b1)
        spread(1, b, two)

    deep = (window + TQ - 2) // TQ
    want_a = jnp.minimum(2 * step, deep) + 1
    want_b = jnp.minimum(2 * step + 1, deep) + 1
    for one, two in ((1, 2), (2, 2), (3, 3), (3, 4), (4, 4)):
        @pl.when((2 * step * TQ < length) & (want_a == one) & (want_b == two))
        def _(one=one, two=two):
            pair(one, two)

    @pl.when(step == steps - 1)
    def _():
        part = tokens // 4
        for k in range(4):
            at = pl.multiple_of(lax.rem(x_id + k, 4) * part, part)
            outs[k][...] = acc[pl.ds(at, part), :].astype(BF)


def attention(scalars, queries, key_rows, out_grad, layers):
    slots, tokens = queries.shape[2], queries.shape[3]
    per_dev = queries.shape[4] // HD
    part = tokens // 4
    wide = per_dev * HD
    row_block = pl.BlockSpec((None, None, None, RB, wide), lambda j, i, *_: (0, 0, j, i, 0))
    key_block = pl.BlockSpec(
        (None, None, None, tokens, HD), lambda j, i, ids, *_: (0, 0, j, 0, ids[2]))
    out_block = pl.BlockSpec((None, part, HD), lambda j, i, *_: (j, 0, 0))
    return pl.pallas_call(
        functools.partial(attention_kernel, layers, tokens, per_dev),
        grid_spec=pltpu.PrefetchScalarGridSpec(
            num_scalar_prefetch=4,
            grid=(slots, tokens // RB),
            in_specs=[row_block, key_block, row_block],
            out_specs=[out_block] * 4,
            scratch_shapes=[
                pltpu.VMEM((tokens, HD), F32),
                pltpu.VMEM((2, tokens // 2 + TQ, per_dev * TQ), BF),
                pltpu.VMEM((2, per_dev * TQ, HD), BF),
            ],
        ),
        out_shape=[jax.ShapeDtypeStruct((slots, part, HD), BF)] * 4,
        compiler_params=pltpu.CompilerParams(vmem_limit_bytes=VMEM),
        cost_estimate=pl.CostEstimate(
            flops=36 * per_dev * 4 * TQ * TQ * HD, bytes_accessed=4 << 20,
            transcendentals=36 * per_dev * TQ * TQ),
        name="attention",
    )(*scalars, queries, key_rows, out_grad)


def grad_kernel(tokens, rows, ids, x_ref, *refs):
    pieces = refs[:4]
    out_ref, value, result = refs[-3:]
    core = lax.rem(ids[1], 2)
    y_id, x_id = ids[2], ids[3]
    part = tokens // 4
    for k in range(4):
        for i in range(4):
            y = lax.rem(y_id + 4 - jnp.where(core == 0, k, i), 4)
            x = lax.rem(x_id + 4 - jnp.where(core == 0, i, k), 4)
            at = pl.multiple_of(x * part, part)
            col = pl.multiple_of(y * HD, HD)
            value[pl.ds(at, part), pl.ds(col, HD)] = pieces[k][i]
    result[...] = lax.dot_general(
        x_ref[...], value[...], (((0,), (0,)), ((), ())), preferred_element_type=F32)
    for z in range(out_ref.shape[0]):
        out_ref[z] = result[z * rows:(z + 1) * rows, :].astype(BF)


def layer_grad(fixed, ids, normed, pieces, rows, earlier):
    slots, tokens, width = normed.shape[2:]
    group = width // rows
    part = tokens // 4
    out_block = pl.BlockSpec((group, None, rows, KVH * HD), lambda i, *_: (0, fixed, 0, 0))
    extra = [] if earlier is None else [earlier]
    return pl.pallas_call(
        functools.partial(grad_kernel, tokens, rows),
        grid_spec=pltpu.PrefetchScalarGridSpec(
            num_scalar_prefetch=1,
            grid=(1,),
            in_specs=[pl.BlockSpec((None, None, None, tokens, width),
                                   lambda i, *_: (0, 0, fixed, 0, 0))]
            + [pl.BlockSpec((4, part, HD), lambda i, *_: (0, 0, 0))] * 4
            + [pl.BlockSpec(memory_space=pl.ANY)] * len(extra),
            out_specs=out_block,
            scratch_shapes=[pltpu.VMEM((tokens, KVH * HD), BF),
                            pltpu.VMEM((width, KVH * HD), F32)],
        ),
        out_shape=jax.ShapeDtypeStruct((group, slots, rows, KVH * HD), BF),
        input_output_aliases={6: 0} if extra else {},
        compiler_params=pltpu.CompilerParams(vmem_limit_bytes=16 << 20),
        cost_estimate=pl.CostEstimate(
            flops=2 * tokens * width * KVH * HD, bytes_accessed=3 << 20, transcendentals=0),
        name="layer_grad%d" % fixed,
    )(ids, normed, *pieces, *extra)


def adam_kernel(reps, sections, layers, batch, lmap, arrived, master, one, two,
                new_master, new_one, new_two, send):
    step = pl.program_id(0)

    @pl.when(step == 0)
    def _():
        send[...] = jnp.zeros_like(send)

    for i in range(batch):
        layer = step * batch + i
        total = None
        places = []
        for r in range(reps):
            section = lmap[r, layer]
            first, _ = first_and_count(lmap, r, section, layers)
            slot = layer - first
            source = r * sections + section
            places.append((source, slot))
            term = arrived[source, slot].astype(F32)
            total = term if total is None else total + term
        mean = total / reps
        m1 = BETA_ONE * one[i] + (1.0 - BETA_ONE) * mean
        m2 = BETA_TWO * two[i] + (1.0 - BETA_TWO) * mean * mean
        move = m1 / CORRECT_ONE / (jnp.sqrt(m2 / CORRECT_TWO) + EPSILON)
        updated = master[i] - LEARN_RATE * (move + DECAY_RATE * master[i])
        new_master[i] = updated
        new_one[i] = m1
        new_two[i] = m2
        rounded = updated.astype(BF)
        for source, slot in places:
            send[source, slot] = rounded


def adam(lmap, arrived, master, one, two):
    layers, _, rows, wide = master.shape
    reps = lmap.shape[0]
    batch = layers // 2
    state = pl.BlockSpec((batch, None, rows, wide), lambda l, *_: (l, 0, 0, 0))
    whole = pl.BlockSpec(arrived.shape, lambda l, *_: (0, 0, 0, 0))
    f32 = jax.ShapeDtypeStruct(master.shape, F32)
    return pl.pallas_call(
        functools.partial(adam_kernel, reps, arrived.shape[0] // reps, layers, batch),
        grid_spec=pltpu.PrefetchScalarGridSpec(
            num_scalar_prefetch=1,
            grid=(layers // batch,),
            in_specs=[whole, state, state, state],
            out_specs=[state, state, state, whole],
        ),
        out_shape=[f32, f32, f32, jax.ShapeDtypeStruct(arrived.shape, BF)],
        compiler_params=pltpu.CompilerParams(vmem_limit_bytes=16 << 20),
        cost_estimate=pl.CostEstimate(flops=20 * master.size, bytes_accessed=4 << 20,
                                      transcendentals=master.size),
        name="adamw",
    )(lmap, arrived, master, one, two)


def place_kernel(arrived, out, sem):
    copies = []
    for i in range(arrived.shape[0]):
        for j in range(arrived.shape[1]):
            copies.append(pltpu.make_async_copy(
                arrived.at[i, j], out.at[j, i], sem.at[len(copies)]))
    for c in copies:
        c.start()
    for c in copies:
        c.wait()


def place(arrived):
    group, slots, rows, wide = arrived.shape
    return pl.pallas_call(
        place_kernel,
        in_specs=[pl.BlockSpec(memory_space=pl.ANY)],
        out_specs=pl.BlockSpec(memory_space=pl.ANY),
        scratch_shapes=[pltpu.SemaphoreType.DMA((group * slots,))],
        out_shape=jax.ShapeDtypeStruct((slots, group, rows, wide), BF),
        compiler_params=pltpu.CompilerParams(vmem_limit_bytes=4 << 20),
        cost_estimate=pl.CostEstimate(flops=0, bytes_accessed=2 << 20, transcendentals=0),
        name="place",
    )(arrived)


def shift(value, axis, by):
    n = lax.axis_size(axis)
    return lax.ppermute(value, axis, [(i, (i + by) % n) for i in range(n)])


def turn(value, by, along_x):
    pairs = []
    for core in range(2):
        for y in range(4):
            for x in range(4):
                if along_x == (core == 0):
                    to = (y, (x + by) % 4)
                else:
                    to = ((y + by) % 4, x)
                pairs.append(((core * 4 + y) * 4 + x, (core * 4 + to[0]) * 4 + to[1]))
    return lax.ppermute(value, ("core", "y", "x"), pairs)


def body(layer_section, token_count, window_size, normed_input, queries, key_rows, out_grad,
         master, moment_one, moment_two):
    layers = layer_section.shape[1]
    group_axes = ("rep", "z", "core")
    ids = jnp.stack([
        lax.axis_index("rep"), lax.axis_index(("z", "core")),
        lax.axis_index("y"), lax.axis_index("x")]).astype(jnp.int32)
    rows = master.shape[2]
    parts = attention((ids, layer_section, token_count, window_size),
                      queries, key_rows, out_grad, layers)
    total = parts[0].astype(F32)
    for k in range(1, 4):
        total = total + shift(parts[k], "x", k).astype(F32)
    block = total.astype(BF)
    near = [block] + [turn(block, k, True) for k in range(1, 4)]
    low, high = jnp.stack([n[0] for n in near]), jnp.stack([n[1] for n in near])
    low_up, high_down = turn(low, 1, False), turn(high, 3, False)
    high_up, low_down = turn(high, 1, False), turn(low, 3, False)
    low_far, high_far = turn(low_up, 1, False), turn(high_down, 3, False)
    grads = layer_grad(0, ids, normed_input, [low, low_up, low_far, low_down], rows, None)
    grads = layer_grad(1, ids, normed_input, [high, high_up, high_far, high_down], rows, grads)
    arrived = lax.all_to_all(grads, group_axes, 0, 0, tiled=True)
    updated, first, second, send = adam(
        layer_section, arrived, master, moment_one, moment_two)
    weights = place(lax.all_to_all(send, group_axes, 0, 0, tiled=True))
    weights = weights.reshape(weights.shape[0], -1, weights.shape[3])
    return updated, first, second, weights[None, None]


def solution(mesh):
    reps, sections, tps = mesh.devices.shape
    fine = Mesh(mesh.devices.reshape(reps, 2, sections // 2, 4, tps // 4),
                ("rep", "z", "core", "y", "x"))
    section, tp = ("z", "core"), ("y", "x")
    wide = P("rep", section, None, None, tp)
    state = P(None, tp, ("rep",) + section, None)
    in_specs = (P(), P(), P(), wide, wide, P("rep", section, None, None, None), wide,
                state, state, state)
    out_specs = (state, state, state, P("rep", section, None, tp, None))
    return jax.shard_map(body, mesh=fine, in_specs=in_specs, out_specs=out_specs, check_vma=False)
```

```python
import functools

import jax
import jax.numpy as jnp
from jax import lax
from jax.experimental import pallas as pl
from jax.experimental.pallas import tpu as pltpu
from jax.sharding import Mesh, PartitionSpec as P

HQ = 32
KVH = 4
HD = 128
BETA_ONE = 0.9
BETA_TWO = 0.95
LEARN_RATE = 0.03
DECAY_RATE = 0.1
EPSILON = 1e-08
CORRECT_ONE = 0.9999734386011124
CORRECT_TWO = 0.994079470779667
LOG2E = 1.4426950408889634
TQ = 256
RB = 1536
VMEM = 60 << 20
BF = jnp.bfloat16
F32 = jnp.float32


def section_index():
    return 2 * lax.axis_index("z") + lax.axis_index("core")


def first_and_count(map_ref, replica, section, layers):
    first = jnp.int32(0)
    count = jnp.int32(0)
    for l in range(layers):
        at = map_ref[replica, l]
        first += (at < section).astype(jnp.int32)
        count += (at == section).astype(jnp.int32)
    return first, count


def attention_kernel(layers, tokens, per_dev, lmap, counts, windows,
                     q_ref, k_ref, g_ref, *rest):
    outs = rest[:4]
    acc, p_scr, g_scr = rest[4:]
    slot, step = pl.program_id(0), pl.program_id(1)
    steps = pl.num_programs(1)
    replica, section, x_id = lax.axis_index("rep"), section_index(), lax.axis_index("x")
    first, held = first_and_count(lmap, replica, section, layers)
    layer = jnp.minimum(first + slot, layers - 1)
    window = windows[layer]
    length = jnp.where(slot < held, counts[replica], 0)
    reach = tokens // 2 // TQ
    scale = HD ** (-0.5) * LOG2E

    @pl.when(step == 0)
    def _():
        acc[...] = jnp.zeros_like(acc)

    diff = (lax.broadcasted_iota(jnp.int32, (TQ, TQ), 1)
            - lax.broadcasted_iota(jnp.int32, (TQ, TQ), 0))

    def scores(sub, index, chunks, h):
        base = pl.multiple_of((index - (chunks - 1)) * TQ, TQ)
        query = q_ref[sub * TQ:(sub + 1) * TQ, h * HD:(h + 1) * HD]
        parts = []
        peak = None
        for c in range(chunks):
            s = lax.dot_general(
                k_ref[pl.ds(base + c * TQ, TQ), :], query, (((1,), (1,)), ((), ())),
                preferred_element_type=F32)
            off = (chunks - 1 - c) * TQ
            ok = None
            if c < 2:
                ok = diff < (window - off)
            if c == chunks - 1:
                ok = diff >= 0 if ok is None else ok & (diff >= 0)
            if ok is not None:
                s = jnp.where(ok, s, -1e30)
            parts.append(s)
            m = jnp.max(s, axis=0, keepdims=True)
            peak = m if peak is None else jnp.maximum(peak, m)
        return parts, peak

    def weigh(sub, index, h, parts, peak):
        shift = peak * scale
        total = None
        for c, s in enumerate(parts):
            e = jnp.exp2(s * scale - shift)
            t = jnp.sum(e, axis=0, keepdims=True)
            total = t if total is None else total + t
            p_scr[sub, c * TQ:(c + 1) * TQ, h * TQ:(h + 1) * TQ] = e.astype(BF)
        live = (index * TQ + lax.broadcasted_iota(jnp.int32, (1, TQ), 1)) < length
        inverse = jnp.where(live, 1.0 / total, 0.0)
        column = jnp.broadcast_to(inverse, (HD, TQ)).T
        grad = g_ref[sub * TQ:(sub + 1) * TQ, h * HD:(h + 1) * HD].astype(F32) * column
        g_scr[sub, h * TQ:(h + 1) * TQ, :] = grad.astype(BF)

    def spread(sub, index, chunks):
        base = pl.multiple_of((index - (chunks - 1)) * TQ, TQ)
        for c in range(chunks):
            acc[pl.ds(base + c * TQ, TQ), :] += jnp.dot(
                p_scr[sub, c * TQ:(c + 1) * TQ, :], g_scr[sub], preferred_element_type=F32)

    def run(counts):
        units = [(sub, h) for sub in range(len(counts)) for h in range(per_dev)]
        ready = {}
        late = []

        def score(u):
            if u < len(units):
                sub, h = units[u]
                ready[u] = scores(sub, len(counts) * step + sub, counts[sub], h)

        for u in range(2):
            score(u)
        for u, (sub, h) in enumerate(units):
            score(u + 2)
            for wait in [w for w in late if w[0] <= u]:
                spread(wait[1], len(counts) * step + wait[1], counts[wait[1]])
                late.remove(wait)
            weigh(sub, len(counts) * step + sub, h, *ready.pop(u))
            if h == per_dev - 1:
                late.append((u + 2, sub))
        for wait in late:
            spread(wait[1], len(counts) * step + wait[1], counts[wait[1]])

    deep = (window + TQ - 2) // TQ
    blocks = RB // TQ
    want = [jnp.minimum(blocks * step + i, deep) + 1 for i in range(blocks)]
    for counts in ((1, 2, 2, 2, 2, 2), (1, 2, 3, 3, 3, 3), (1, 2, 3, 4, 4, 4)):
        match = blocks * step * TQ < length
        for w, c in zip(want, counts):
            match = match & (w == c)

        @pl.when(match)
        def _(counts=counts):
            run(counts)

    @pl.when(step == steps - 1)
    def _():
        part = tokens // 4
        for k in range(4):
            at = pl.multiple_of(lax.rem(x_id + k, 4) * part, part)
            outs[k][...] = acc[pl.ds(at, part), :].astype(BF)


def attention(scalars, queries, key_rows, out_grad, layers):
    slots, tokens = queries.shape[2], queries.shape[3]
    per_dev = queries.shape[4] // HD
    part = tokens // 4
    wide = per_dev * HD
    row_block = pl.BlockSpec((None, None, None, RB, wide), lambda j, i, *_: (0, 0, j, i, 0))
    key_block = pl.BlockSpec(
        (None, None, None, tokens, HD), lambda j, i, *_: (0, 0, j, 0, lax.axis_index("y")))
    out_block = pl.BlockSpec((None, part, HD), lambda j, i, *_: (j, 0, 0))
    return pl.pallas_call(
        functools.partial(attention_kernel, layers, tokens, per_dev),
        grid_spec=pltpu.PrefetchScalarGridSpec(
            num_scalar_prefetch=3,
            grid=(slots, tokens // RB),
            in_specs=[row_block, key_block, row_block],
            out_specs=[out_block] * 4,
            scratch_shapes=[
                pltpu.VMEM((tokens, HD), F32),
                pltpu.VMEM((6, tokens // 2 + TQ, per_dev * TQ), BF),
                pltpu.VMEM((6, per_dev * TQ, HD), BF),
            ],
        ),
        out_shape=[jax.ShapeDtypeStruct((slots, part, HD), BF)] * 4,
        compiler_params=pltpu.CompilerParams(vmem_limit_bytes=VMEM),
        cost_estimate=pl.CostEstimate(
            flops=36 * per_dev * 4 * TQ * TQ * HD, bytes_accessed=4 << 20,
            transcendentals=36 * per_dev * TQ * TQ),
        name="attention",
    )(*scalars, queries, key_rows, out_grad)


def grad_kernel(tokens, rows, x_ref, *refs):
    out_ref, value, result = refs[-3:]
    core, y_id, x_id = (lax.axis_index(n) for n in ("core", "y", "x"))
    part = tokens // 4
    for slot in range(2):
        @pl.when(pl.program_id(0) == slot)
        def _(pieces=refs[4 * slot:4 * slot + 4]):
            for k in range(4):
                for i in range(4):
                    y = lax.rem(y_id + 4 - jnp.where(core == 0, k, i), 4)
                    x = lax.rem(x_id + 4 - jnp.where(core == 0, i, k), 4)
                    at = pl.multiple_of(x * part, part)
                    col = pl.multiple_of(y * HD, HD)
                    value[pl.ds(at, part), pl.ds(col, HD)] = pieces[k][i]

    result[...] = lax.dot_general(
        x_ref[...], value[...], (((0,), (0,)), ((), ())), preferred_element_type=F32)
    for z in range(out_ref.shape[0]):
        out_ref[z] = result[z * rows:(z + 1) * rows, :].astype(BF)


def layer_grads(normed, low, high, rows):
    slots, tokens, width = normed.shape[2:]
    group = width // rows
    part = tokens // 4
    out_block = pl.BlockSpec((group, None, rows, KVH * HD), lambda j, *_: (0, j, 0, 0))
    return pl.pallas_call(
        functools.partial(grad_kernel, tokens, rows),
        grid_spec=pltpu.PrefetchScalarGridSpec(
            num_scalar_prefetch=0,
            grid=(slots,),
            in_specs=[pl.BlockSpec((None, None, None, tokens, width),
                                   lambda j, *_: (0, 0, j, 0, 0))]
            + [pl.BlockSpec((4, part, HD), lambda j, *_: (0, 0, 0))] * 8,
            out_specs=out_block,
            scratch_shapes=[pltpu.VMEM((tokens, KVH * HD), BF),
                            pltpu.VMEM((width, KVH * HD), F32)],
        ),
        out_shape=jax.ShapeDtypeStruct((group, slots, rows, KVH * HD), BF),
        compiler_params=pltpu.CompilerParams(vmem_limit_bytes=16 << 20),
        cost_estimate=pl.CostEstimate(
            flops=4 * tokens * width * KVH * HD, bytes_accessed=6 << 20, transcendentals=0),
        name="layer_grads",
    )(normed, *low, *high)


def adam_kernel(reps, sections, layers, batch, lmap, arrived, master, one, two,
                new_master, new_one, new_two, send):
    step = pl.program_id(0)

    @pl.when(step == 0)
    def _():
        send[...] = jnp.zeros_like(send)

    for i in range(batch):
        layer = step * batch + i
        total = None
        places = []
        for r in range(reps):
            section = lmap[r, layer]
            first, _ = first_and_count(lmap, r, section, layers)
            slot = layer - first
            source = r * sections + section
            places.append((source, slot))
            term = arrived[source, slot].astype(F32)
            total = term if total is None else total + term
        mean = total / reps
        m1 = BETA_ONE * one[i] + (1.0 - BETA_ONE) * mean
        m2 = BETA_TWO * two[i] + (1.0 - BETA_TWO) * mean * mean
        move = m1 / CORRECT_ONE / (jnp.sqrt(m2 / CORRECT_TWO) + EPSILON)
        updated = master[i] - LEARN_RATE * (move + DECAY_RATE * master[i])
        new_master[i] = updated
        new_one[i] = m1
        new_two[i] = m2
        rounded = updated.astype(BF)
        for source, slot in places:
            send[source, slot] = rounded


def adam(lmap, arrived, master, one, two):
    layers, _, rows, wide = master.shape
    reps = lmap.shape[0]
    batch = layers // 2
    state = pl.BlockSpec((batch, None, rows, wide), lambda l, *_: (l, 0, 0, 0))
    whole = pl.BlockSpec(arrived.shape, lambda l, *_: (0, 0, 0, 0))
    f32 = jax.ShapeDtypeStruct(master.shape, F32)
    return pl.pallas_call(
        functools.partial(adam_kernel, reps, arrived.shape[0] // reps, layers, batch),
        grid_spec=pltpu.PrefetchScalarGridSpec(
            num_scalar_prefetch=1,
            grid=(layers // batch,),
            in_specs=[whole, state, state, state],
            out_specs=[state, state, state, whole],
        ),
        out_shape=[f32, f32, f32, jax.ShapeDtypeStruct(arrived.shape, BF)],
        compiler_params=pltpu.CompilerParams(vmem_limit_bytes=16 << 20),
        cost_estimate=pl.CostEstimate(flops=20 * master.size, bytes_accessed=4 << 20,
                                      transcendentals=master.size),
        name="adamw",
    )(lmap, arrived, master, one, two)


def place_kernel(arrived, out, sem):
    copies = []
    for i in range(arrived.shape[0]):
        for j in range(arrived.shape[1]):
            copies.append(pltpu.make_async_copy(
                arrived.at[i, j], out.at[j, i], sem.at[len(copies)]))
    for c in copies:
        c.start()
    for c in copies:
        c.wait()


def place(arrived):
    group, slots, rows, wide = arrived.shape
    return pl.pallas_call(
        place_kernel,
        in_specs=[pl.BlockSpec(memory_space=pl.ANY)],
        out_specs=pl.BlockSpec(memory_space=pl.ANY),
        scratch_shapes=[pltpu.SemaphoreType.DMA((group * slots,))],
        out_shape=jax.ShapeDtypeStruct((slots, group, rows, wide), BF),
        compiler_params=pltpu.CompilerParams(vmem_limit_bytes=4 << 20),
        cost_estimate=pl.CostEstimate(flops=0, bytes_accessed=2 << 20, transcendentals=0),
        name="place",
    )(arrived)


def shift(value, axis, by):
    n = lax.axis_size(axis)
    return lax.ppermute(value, axis, [(i, (i + by) % n) for i in range(n)])


def turn(value, by, along_x):
    pairs = []
    for core in range(2):
        for y in range(4):
            for x in range(4):
                if along_x == (core == 0):
                    to = (y, (x + by) % 4)
                else:
                    to = ((y + by) % 4, x)
                pairs.append(((core * 4 + y) * 4 + x, (core * 4 + to[0]) * 4 + to[1]))
    return lax.ppermute(value, ("core", "y", "x"), pairs)


def body(layer_section, token_count, window_size, normed_input, queries, key_rows, out_grad,
         master, moment_one, moment_two):
    layers = layer_section.shape[1]
    group_axes = ("rep", "z", "core")
    rows = master.shape[2]
    parts = attention((layer_section, token_count, window_size),
                      queries, key_rows, out_grad, layers)
    total = parts[0].astype(F32)
    for k in range(1, 4):
        total = total + shift(parts[k], "x", k).astype(F32)
    block = total.astype(BF)
    near = [block] + [turn(block, k, True) for k in range(1, 4)]
    low, high = jnp.stack([n[0] for n in near]), jnp.stack([n[1] for n in near])
    low_up, high_down = turn(low, 1, False), turn(high, 3, False)
    high_up, low_down = turn(high, 1, False), turn(low, 3, False)
    low_far, high_far = turn(low_up, 1, False), turn(high_down, 3, False)
    grads = layer_grads(normed_input, [low, low_up, low_far, low_down],
                        [high, high_up, high_far, high_down], rows)
    arrived = lax.all_to_all(grads, group_axes, 0, 0, tiled=True)
    updated, first, second, send = adam(
        layer_section, arrived, master, moment_one, moment_two)
    weights = place(lax.all_to_all(send, group_axes, 0, 0, tiled=True))
    weights = weights.reshape(weights.shape[0], -1, weights.shape[3])
    return updated, first, second, weights[None, None]


def solution(mesh):
    reps, sections, tps = mesh.devices.shape
    fine = Mesh(mesh.devices.reshape(reps, 2, sections // 2, 4, tps // 4),
                ("rep", "z", "core", "y", "x"))
    section, tp = ("z", "core"), ("y", "x")
    wide = P("rep", section, None, None, tp)
    state = P(None, tp, ("rep",) + section, None)
    in_specs = (P(), P(), P(), wide, wide, P("rep", section, None, None, None), wide,
                state, state, state)
    out_specs = (state, state, state, P("rep", section, None, tp, None))
    return jax.shard_map(body, mesh=fine, in_specs=in_specs, out_specs=out_specs, check_vma=False)
```

```python
import functools

import jax
import jax.numpy as jnp
from jax import lax
from jax.experimental import pallas as pl
from jax.experimental.pallas import tpu as pltpu
from jax.sharding import Mesh, PartitionSpec as P

HQ = 32
KVH = 4
HD = 128
BETA_ONE = 0.9
BETA_TWO = 0.95
LEARN_RATE = 0.03
DECAY_RATE = 0.1
EPSILON = 1e-08
CORRECT_ONE = 0.9999734386011124
CORRECT_TWO = 0.994079470779667
LOG2E = 1.4426950408889634
TQ = 256
RB = 1536
VMEM = 60 << 20
BF = jnp.bfloat16
F32 = jnp.float32


def section_index():
    return 2 * lax.axis_index("z") + lax.axis_index("core")


def first_and_count(map_ref, replica, section, layers):
    first = jnp.int32(0)
    count = jnp.int32(0)
    for l in range(layers):
        at = map_ref[replica, l]
        first += (at < section).astype(jnp.int32)
        count += (at == section).astype(jnp.int32)
    return first, count


def attention_kernel(layers, tokens, per_dev, lmap, counts, windows,
                     q_ref, k_ref, g_ref, *rest):
    outs = rest[:4]
    flag, acc, p_scr, g_scr = rest[4:]
    slot, step = pl.program_id(0), pl.program_id(1)
    steps = pl.num_programs(1)
    replica, section, x_id = lax.axis_index("rep"), section_index(), lax.axis_index("x")
    first, held = first_and_count(lmap, replica, section, layers)
    flag[0] = held
    layer = jnp.minimum(first + slot, layers - 1)
    window = windows[layer]
    length = jnp.where(slot < held, counts[replica], 0)
    reach = tokens // 2 // TQ
    scale = HD ** (-0.5) * LOG2E

    @pl.when(step == 0)
    def _():
        acc[...] = jnp.zeros_like(acc)

    diff = (lax.broadcasted_iota(jnp.int32, (TQ, TQ), 1)
            - lax.broadcasted_iota(jnp.int32, (TQ, TQ), 0))

    def scores(sub, index, chunks, h):
        base = pl.multiple_of((index - (chunks - 1)) * TQ, TQ)
        query = q_ref[sub * TQ:(sub + 1) * TQ, h * HD:(h + 1) * HD]
        parts = []
        peak = None
        for c in range(chunks):
            s = lax.dot_general(
                k_ref[pl.ds(base + c * TQ, TQ), :], query, (((1,), (1,)), ((), ())),
                preferred_element_type=F32)
            off = (chunks - 1 - c) * TQ
            ok = None
            if c < 2:
                ok = diff < (window - off)
            if c == chunks - 1:
                ok = diff >= 0 if ok is None else ok & (diff >= 0)
            if ok is not None:
                s = jnp.where(ok, s, -1e30)
            parts.append(s)
            m = jnp.max(s, axis=0, keepdims=True)
            peak = m if peak is None else jnp.maximum(peak, m)
        return parts, peak

    def weigh(sub, index, h, parts, peak):
        shift = peak * scale
        total = None
        for c, s in enumerate(parts):
            e = jnp.exp2(s * scale - shift)
            t = jnp.sum(e, axis=0, keepdims=True)
            total = t if total is None else total + t
            p_scr[sub, c * TQ:(c + 1) * TQ, h * TQ:(h + 1) * TQ] = e.astype(BF)
        live = (index * TQ + lax.broadcasted_iota(jnp.int32, (1, TQ), 1)) < length
        inverse = jnp.where(live, 1.0 / total, 0.0)
        column = jnp.broadcast_to(inverse, (HD, TQ)).T
        grad = g_ref[sub * TQ:(sub + 1) * TQ, h * HD:(h + 1) * HD].astype(F32) * column
        g_scr[sub, h * TQ:(h + 1) * TQ, :] = grad.astype(BF)

    def spread(sub, index, chunks):
        base = pl.multiple_of((index - (chunks - 1)) * TQ, TQ)
        for c in range(chunks):
            acc[pl.ds(base + c * TQ, TQ), :] += jnp.dot(
                p_scr[sub, c * TQ:(c + 1) * TQ, :], g_scr[sub], preferred_element_type=F32)

    def run(counts):
        units = [(sub, h) for sub in range(len(counts)) for h in range(per_dev)]
        ready = {}
        late = []

        def score(u):
            if u < len(units):
                sub, h = units[u]
                ready[u] = scores(sub, len(counts) * step + sub, counts[sub], h)

        for u in range(2):
            score(u)
        for u, (sub, h) in enumerate(units):
            score(u + 2)
            for wait in [w for w in late if w[0] <= u]:
                spread(wait[1], len(counts) * step + wait[1], counts[wait[1]])
                late.remove(wait)
            weigh(sub, len(counts) * step + sub, h, *ready.pop(u))
            if h == per_dev - 1:
                late.append((u + 2, sub))
        for wait in late:
            spread(wait[1], len(counts) * step + wait[1], counts[wait[1]])

    deep = (window + TQ - 2) // TQ
    blocks = RB // TQ
    want = [jnp.minimum(blocks * step + i, deep) + 1 for i in range(blocks)]
    for counts in ((1, 2, 2, 2, 2, 2), (1, 2, 3, 3, 3, 3), (1, 2, 3, 4, 4, 4)):
        match = blocks * step * TQ < length
        for w, c in zip(want, counts):
            match = match & (w == c)

        @pl.when(match)
        def _(counts=counts):
            run(counts)

    @pl.when(step == steps - 1)
    def _():
        part = tokens // 4
        for k in range(4):
            at = pl.multiple_of(lax.rem(x_id + k, 4) * part, part)
            outs[k][...] = acc[pl.ds(at, part), :].astype(BF)


def attention(scalars, queries, key_rows, out_grad, layers):
    slots, tokens = queries.shape[2], queries.shape[3]
    per_dev = queries.shape[4] // HD
    part = tokens // 4
    wide = per_dev * HD
    row_block = pl.BlockSpec((None, None, None, RB, wide), lambda j, i, *_: (0, 0, j, i, 0))
    key_block = pl.BlockSpec(
        (None, None, None, tokens, HD), lambda j, i, *_: (0, 0, j, 0, lax.axis_index("y")))
    out_block = pl.BlockSpec((None, part, HD), lambda j, i, *_: (j, 0, 0))
    return pl.pallas_call(
        functools.partial(attention_kernel, layers, tokens, per_dev),
        grid_spec=pltpu.PrefetchScalarGridSpec(
            num_scalar_prefetch=3,
            grid=(slots, tokens // RB),
            in_specs=[row_block, key_block, row_block],
            out_specs=[out_block] * 4 + [pl.BlockSpec(memory_space=pltpu.SMEM)],
            scratch_shapes=[
                pltpu.VMEM((tokens, HD), F32),
                pltpu.VMEM((6, tokens // 2 + TQ, per_dev * TQ), BF),
                pltpu.VMEM((6, per_dev * TQ, HD), BF),
            ],
        ),
        out_shape=[jax.ShapeDtypeStruct((slots, part, HD), BF)] * 4
        + [jax.ShapeDtypeStruct((1,), jnp.int32)],
        compiler_params=pltpu.CompilerParams(vmem_limit_bytes=VMEM),
        cost_estimate=pl.CostEstimate(
            flops=36 * per_dev * 4 * TQ * TQ * HD, bytes_accessed=4 << 20,
            transcendentals=36 * per_dev * TQ * TQ),
        name="attention",
    )(*scalars, queries, key_rows, out_grad)


def grad_slot(tokens, rows, x_ref, pieces, out_ref, value, result):
    core, y_id, x_id = (lax.axis_index(n) for n in ("core", "y", "x"))
    part = tokens // 4
    for k in range(4):
        for i in range(4):
            y = lax.rem(y_id + 4 - jnp.where(core == 0, k, i), 4)
            x = lax.rem(x_id + 4 - jnp.where(core == 0, i, k), 4)
            at = pl.multiple_of(x * part, part)
            col = pl.multiple_of(y * HD, HD)
            value[pl.ds(at, part), pl.ds(col, HD)] = pieces[k][i]
    result[...] = lax.dot_general(
        x_ref[...], value[...], (((0,), (0,)), ((), ())), preferred_element_type=F32)
    for z in range(out_ref.shape[0]):
        out_ref[z] = result[z * rows:(z + 1) * rows, :].astype(BF)


def grad_kernel(tokens, rows, x_ref, *refs):
    for slot in range(2):
        @pl.when(pl.program_id(0) == slot)
        def _(pieces=refs[4 * slot:4 * slot + 4]):
            grad_slot(tokens, rows, x_ref, pieces, *refs[8:])


def first_kernel(tokens, rows, x_ref, *refs):
    out_ref = refs[4]
    grad_slot(tokens, rows, x_ref, refs[:4], out_ref.at[:, 0], *refs[5:])
    out_ref[:, 1] = jnp.zeros(out_ref.shape[:1] + out_ref.shape[2:], BF)


def first_grad(normed, low, rows):
    slots, tokens, width = normed.shape[2:]
    group = width // rows
    part = tokens // 4
    return pl.pallas_call(
        functools.partial(first_kernel, tokens, rows),
        grid=(1,),
        in_specs=[pl.BlockSpec((None, None, None, tokens, width), lambda j: (0, 0, 0, 0, 0))]
        + [pl.BlockSpec((4, part, HD), lambda j: (0, 0, 0))] * 4,
        out_specs=pl.BlockSpec((group, slots, rows, KVH * HD), lambda j: (0, 0, 0, 0)),
        scratch_shapes=[pltpu.VMEM((tokens, KVH * HD), BF),
                        pltpu.VMEM((width, KVH * HD), F32)],
        out_shape=jax.ShapeDtypeStruct((group, slots, rows, KVH * HD), BF),
        compiler_params=pltpu.CompilerParams(vmem_limit_bytes=16 << 20),
        cost_estimate=pl.CostEstimate(
            flops=2 * tokens * width * KVH * HD, bytes_accessed=3 << 20, transcendentals=0),
        name="first_grad",
    )(normed, *low)


def layer_grads(normed, low, high, rows):
    slots, tokens, width = normed.shape[2:]
    group = width // rows
    part = tokens // 4
    out_block = pl.BlockSpec((group, None, rows, KVH * HD), lambda j, *_: (0, j, 0, 0))
    return pl.pallas_call(
        functools.partial(grad_kernel, tokens, rows),
        grid_spec=pltpu.PrefetchScalarGridSpec(
            num_scalar_prefetch=0,
            grid=(slots,),
            in_specs=[pl.BlockSpec((None, None, None, tokens, width),
                                   lambda j, *_: (0, 0, j, 0, 0))]
            + [pl.BlockSpec((4, part, HD), lambda j, *_: (0, 0, 0))] * 8,
            out_specs=out_block,
            scratch_shapes=[pltpu.VMEM((tokens, KVH * HD), BF),
                            pltpu.VMEM((width, KVH * HD), F32)],
        ),
        out_shape=jax.ShapeDtypeStruct((group, slots, rows, KVH * HD), BF),
        compiler_params=pltpu.CompilerParams(vmem_limit_bytes=16 << 20),
        cost_estimate=pl.CostEstimate(
            flops=4 * tokens * width * KVH * HD, bytes_accessed=6 << 20, transcendentals=0),
        name="layer_grads",
    )(normed, *low, *high)


def adam_kernel(reps, sections, layers, batch, lmap, arrived, master, one, two,
                new_master, new_one, new_two, send):
    step = pl.program_id(0)

    @pl.when(step == 0)
    def _():
        send[...] = jnp.zeros_like(send)

    for i in range(batch):
        layer = step * batch + i
        total = None
        places = []
        for r in range(reps):
            section = lmap[r, layer]
            first, _ = first_and_count(lmap, r, section, layers)
            slot = layer - first
            source = r * sections + section
            places.append((source, slot))
            term = arrived[source, slot].astype(F32)
            total = term if total is None else total + term
        mean = total / reps
        m1 = BETA_ONE * one[i] + (1.0 - BETA_ONE) * mean
        m2 = BETA_TWO * two[i] + (1.0 - BETA_TWO) * mean * mean
        move = m1 / CORRECT_ONE / (jnp.sqrt(m2 / CORRECT_TWO) + EPSILON)
        updated = master[i] - LEARN_RATE * (move + DECAY_RATE * master[i])
        new_master[i] = updated
        new_one[i] = m1
        new_two[i] = m2
        rounded = updated.astype(BF)
        for source, slot in places:
            send[source, slot] = rounded


def adam(lmap, arrived, master, one, two):
    layers, _, rows, wide = master.shape
    reps = lmap.shape[0]
    batch = layers // 2
    state = pl.BlockSpec((batch, None, rows, wide), lambda l, *_: (l, 0, 0, 0))
    whole = pl.BlockSpec(arrived.shape, lambda l, *_: (0, 0, 0, 0))
    f32 = jax.ShapeDtypeStruct(master.shape, F32)
    return pl.pallas_call(
        functools.partial(adam_kernel, reps, arrived.shape[0] // reps, layers, batch),
        grid_spec=pltpu.PrefetchScalarGridSpec(
            num_scalar_prefetch=1,
            grid=(layers // batch,),
            in_specs=[whole, state, state, state],
            out_specs=[state, state, state, whole],
        ),
        out_shape=[f32, f32, f32, jax.ShapeDtypeStruct(arrived.shape, BF)],
        compiler_params=pltpu.CompilerParams(vmem_limit_bytes=16 << 20),
        cost_estimate=pl.CostEstimate(flops=20 * master.size, bytes_accessed=4 << 20,
                                      transcendentals=master.size),
        name="adamw",
    )(lmap, arrived, master, one, two)


def place_kernel(arrived, out, sem):
    copies = []
    for i in range(arrived.shape[0]):
        for j in range(arrived.shape[1]):
            copies.append(pltpu.make_async_copy(
                arrived.at[i, j], out.at[j, i], sem.at[len(copies)]))
    for c in copies:
        c.start()
    for c in copies:
        c.wait()


def place(arrived):
    group, slots, rows, wide = arrived.shape
    return pl.pallas_call(
        place_kernel,
        in_specs=[pl.BlockSpec(memory_space=pl.ANY)],
        out_specs=pl.BlockSpec(memory_space=pl.ANY),
        scratch_shapes=[pltpu.SemaphoreType.DMA((group * slots,))],
        out_shape=jax.ShapeDtypeStruct((slots, group, rows, wide), BF),
        compiler_params=pltpu.CompilerParams(vmem_limit_bytes=4 << 20),
        cost_estimate=pl.CostEstimate(flops=0, bytes_accessed=2 << 20, transcendentals=0),
        name="place",
    )(arrived)


def shift(value, axis, by):
    n = lax.axis_size(axis)
    return lax.ppermute(value, axis, [(i, (i + by) % n) for i in range(n)])


def turn(value, by, along_x):
    pairs = []
    for core in range(2):
        for y in range(4):
            for x in range(4):
                if along_x == (core == 0):
                    to = (y, (x + by) % 4)
                else:
                    to = ((y + by) % 4, x)
                pairs.append(((core * 4 + y) * 4 + x, (core * 4 + to[0]) * 4 + to[1]))
    return lax.ppermute(value, ("core", "y", "x"), pairs)


def across(parts):
    total = parts[0].astype(F32)
    for k in range(1, 4):
        total = total + shift(parts[k], "x", k).astype(F32)
    return total.astype(BF)


def body(layer_section, token_count, window_size, normed_input, queries, key_rows, out_grad,
         master, moment_one, moment_two):
    layers = layer_section.shape[1]
    group_axes = ("rep", "z", "core")
    rows = master.shape[2]
    *parts, held = attention((layer_section, token_count, window_size),
                             queries, key_rows, out_grad, layers)

    def both_slots():
        block = across(parts)
        near = [block] + [turn(block, k, True) for k in range(1, 4)]
        low, high = jnp.stack([n[0] for n in near]), jnp.stack([n[1] for n in near])
        low_up, high_down = turn(low, 1, False), turn(high, 3, False)
        high_up, low_down = turn(high, 1, False), turn(low, 3, False)
        low_far, high_far = turn(low_up, 1, False), turn(high_down, 3, False)
        return layer_grads(normed_input, [low, low_up, low_far, low_down],
                           [high, high_up, high_far, high_down], rows)

    def one_slot():
        block = across([p[0] for p in parts])
        low = jnp.stack([block] + [turn(block, k, True) for k in range(1, 4)])
        low_up, low_down = turn(low, 1, False), turn(low, 3, False)
        return first_grad(normed_input, [low, low_up, turn(low_up, 1, False), low_down], rows)

    grads = lax.cond(held[0] == 2, both_slots, one_slot)
    arrived = lax.all_to_all(grads, group_axes, 0, 0, tiled=True)
    updated, first, second, send = adam(
        layer_section, arrived, master, moment_one, moment_two)
    weights = place(lax.all_to_all(send, group_axes, 0, 0, tiled=True))
    weights = weights.reshape(weights.shape[0], -1, weights.shape[3])
    return updated, first, second, weights[None, None]


def solution(mesh):
    reps, sections, tps = mesh.devices.shape
    fine = Mesh(mesh.devices.reshape(reps, 2, sections // 2, 4, tps // 4),
                ("rep", "z", "core", "y", "x"))
    section, tp = ("z", "core"), ("y", "x")
    wide = P("rep", section, None, None, tp)
    state = P(None, tp, ("rep",) + section, None)
    in_specs = (P(), P(), P(), wide, wide, P("rep", section, None, None, None), wide,
                state, state, state)
    out_specs = (state, state, state, P("rep", section, None, tp, None))
    return jax.shard_map(body, mesh=fine, in_specs=in_specs, out_specs=out_specs, check_vma=False)
```

```python
import functools

import jax
import jax.numpy as jnp
from jax import lax
from jax.experimental import pallas as pl
from jax.experimental.pallas import tpu as pltpu
from jax.sharding import Mesh, PartitionSpec as P

HQ = 32
KVH = 4
HD = 128
BETA_ONE = 0.9
BETA_TWO = 0.95
LEARN_RATE = 0.03
DECAY_RATE = 0.1
EPSILON = 1e-08
CORRECT_ONE = 0.9999734386011124
CORRECT_TWO = 0.994079470779667
LOG2E = 1.4426950408889634
TQ = 256
RB = 1536
VMEM = 60 << 20
BF = jnp.bfloat16
F32 = jnp.float32


def section_index():
    return 2 * lax.axis_index("z") + lax.axis_index("core")


def first_and_count(map_ref, replica, section, layers):
    first = jnp.int32(0)
    count = jnp.int32(0)
    for l in range(layers):
        at = map_ref[replica, l]
        first += (at < section).astype(jnp.int32)
        count += (at == section).astype(jnp.int32)
    return first, count


def attention_kernel(layers, tokens, per_dev, lmap, counts, windows,
                     q_ref, k_ref, g_ref, *rest):
    outs = rest[:4]
    flag, acc, p_scr, g_scr = rest[4:]
    slot, step = pl.program_id(0), pl.program_id(1)
    steps = pl.num_programs(1)
    replica, section, x_id = lax.axis_index("rep"), section_index(), lax.axis_index("x")
    first, held = first_and_count(lmap, replica, section, layers)
    flag[0] = held
    layer = jnp.minimum(first + slot, layers - 1)
    window = windows[layer]
    length = jnp.where(slot < held, counts[replica], 0)
    reach = tokens // 2 // TQ
    scale = HD ** (-0.5) * LOG2E

    @pl.when(step == 0)
    def _():
        acc[...] = jnp.zeros_like(acc)

    diff = (lax.broadcasted_iota(jnp.int32, (TQ, TQ), 1)
            - lax.broadcasted_iota(jnp.int32, (TQ, TQ), 0))

    def scores(sub, index, chunks, h):
        base = pl.multiple_of((index - (chunks - 1)) * TQ, TQ)
        query = q_ref[sub * TQ:(sub + 1) * TQ, h * HD:(h + 1) * HD]
        parts = []
        peak = None
        for c in range(chunks):
            s = lax.dot_general(
                k_ref[pl.ds(base + c * TQ, TQ), :], query, (((1,), (1,)), ((), ())),
                preferred_element_type=F32)
            off = (chunks - 1 - c) * TQ
            ok = None
            if c < 2:
                ok = diff < (window - off)
            if c == chunks - 1:
                ok = diff >= 0 if ok is None else ok & (diff >= 0)
            if ok is not None:
                s = jnp.where(ok, s, -1e30)
            parts.append(s)
            m = jnp.max(s, axis=0, keepdims=True)
            peak = m if peak is None else jnp.maximum(peak, m)
        return parts, peak

    def weigh(sub, index, h, parts, peak):
        shift = peak * scale
        total = None
        for c, s in enumerate(parts):
            e = jnp.exp2(s * scale - shift)
            t = jnp.sum(e, axis=0, keepdims=True)
            total = t if total is None else total + t
            p_scr[sub, c * TQ:(c + 1) * TQ, h * TQ:(h + 1) * TQ] = e.astype(BF)
        live = (index * TQ + lax.broadcasted_iota(jnp.int32, (1, TQ), 1)) < length
        inverse = jnp.where(live, 1.0 / total, 0.0)
        column = jnp.broadcast_to(inverse, (HD, TQ)).T
        grad = g_ref[sub * TQ:(sub + 1) * TQ, h * HD:(h + 1) * HD].astype(F32) * column
        g_scr[sub, h * TQ:(h + 1) * TQ, :] = grad.astype(BF)

    def spread(sub, index, chunks):
        base = pl.multiple_of((index - (chunks - 1)) * TQ, TQ)
        for c in range(chunks):
            acc[pl.ds(base + c * TQ, TQ), :] += jnp.dot(
                p_scr[sub, c * TQ:(c + 1) * TQ, :], g_scr[sub], preferred_element_type=F32)

    def run(counts):
        units = [(sub, h) for sub in range(len(counts)) for h in range(per_dev)]
        ready = {}
        late = []

        def score(u):
            if u < len(units):
                sub, h = units[u]
                ready[u] = scores(sub, len(counts) * step + sub, counts[sub], h)

        for u in range(2):
            score(u)
        for u, (sub, h) in enumerate(units):
            score(u + 2)
            for wait in [w for w in late if w[0] <= u]:
                spread(wait[1], len(counts) * step + wait[1], counts[wait[1]])
                late.remove(wait)
            weigh(sub, len(counts) * step + sub, h, *ready.pop(u))
            if h == per_dev - 1:
                late.append((u + 2, sub))
        for wait in late:
            spread(wait[1], len(counts) * step + wait[1], counts[wait[1]])

    deep = (window + TQ - 2) // TQ
    blocks = RB // TQ
    want = [jnp.minimum(blocks * step + i, deep) + 1 for i in range(blocks)]
    for counts in ((1, 2, 2, 2, 2, 2), (1, 2, 3, 3, 3, 3), (1, 2, 3, 4, 4, 4)):
        match = blocks * step * TQ < length
        for w, c in zip(want, counts):
            match = match & (w == c)

        @pl.when(match)
        def _(counts=counts):
            run(counts)

    @pl.when(step == steps - 1)
    def _():
        part = tokens // 4
        for k in range(4):
            at = pl.multiple_of(lax.rem(x_id + k, 4) * part, part)
            outs[k][...] = acc[pl.ds(at, part), :].astype(BF)


def attention(scalars, queries, key_rows, out_grad, layers):
    slots, tokens = queries.shape[2], queries.shape[3]
    per_dev = queries.shape[4] // HD
    part = tokens // 4
    wide = per_dev * HD
    row_block = pl.BlockSpec((None, None, None, RB, wide), lambda j, i, *_: (0, 0, j, i, 0))
    key_block = pl.BlockSpec(
        (None, None, None, tokens, HD), lambda j, i, *_: (0, 0, j, 0, lax.axis_index("y")))
    out_block = pl.BlockSpec((None, part, HD), lambda j, i, *_: (j, 0, 0))
    return pl.pallas_call(
        functools.partial(attention_kernel, layers, tokens, per_dev),
        grid_spec=pltpu.PrefetchScalarGridSpec(
            num_scalar_prefetch=3,
            grid=(slots, tokens // RB),
            in_specs=[row_block, key_block, row_block],
            out_specs=[out_block] * 4 + [pl.BlockSpec(memory_space=pltpu.SMEM)],
            scratch_shapes=[
                pltpu.VMEM((tokens, HD), F32),
                pltpu.VMEM((6, tokens // 2 + TQ, per_dev * TQ), BF),
                pltpu.VMEM((6, per_dev * TQ, HD), BF),
            ],
        ),
        out_shape=[jax.ShapeDtypeStruct((slots, part, HD), BF)] * 4
        + [jax.ShapeDtypeStruct((1,), jnp.int32)],
        compiler_params=pltpu.CompilerParams(vmem_limit_bytes=VMEM),
        cost_estimate=pl.CostEstimate(
            flops=36 * per_dev * 4 * TQ * TQ * HD, bytes_accessed=4 << 20,
            transcendentals=36 * per_dev * TQ * TQ),
        name="attention",
    )(*scalars, queries, key_rows, out_grad)


def grad_slot(tokens, rows, x_ref, pieces, out_ref, value, result):
    core, y_id, x_id = (lax.axis_index(n) for n in ("core", "y", "x"))
    part = tokens // 4
    for k in range(4):
        for i in range(4):
            y = lax.rem(y_id + 4 - jnp.where(core == 0, k, i), 4)
            x = lax.rem(x_id + 4 - jnp.where(core == 0, i, k), 4)
            at = pl.multiple_of(x * part, part)
            col = pl.multiple_of(y * HD, HD)
            value[pl.ds(at, part), pl.ds(col, HD)] = pieces[k][i]
    result[...] = lax.dot_general(
        x_ref[...], value[...], (((0,), (0,)), ((), ())), preferred_element_type=F32)
    for z in range(out_ref.shape[0]):
        out_ref[z] = result[z * rows:(z + 1) * rows, :].astype(BF)


def grad_kernel(tokens, rows, x_ref, *refs):
    for slot in range(2):
        @pl.when(pl.program_id(0) == slot)
        def _(pieces=refs[4 * slot:4 * slot + 4]):
            grad_slot(tokens, rows, x_ref, pieces, *refs[8:])


def first_kernel(tokens, rows, x_ref, *refs):
    out_ref = refs[4]
    grad_slot(tokens, rows, x_ref, refs[:4], out_ref.at[:, 0], *refs[5:])
    out_ref[:, 1] = jnp.zeros(out_ref.shape[:1] + out_ref.shape[2:], BF)


def first_grad(normed, low, rows):
    slots, tokens, width = normed.shape[2:]
    group = width // rows
    part = tokens // 4
    return pl.pallas_call(
        functools.partial(first_kernel, tokens, rows),
        grid=(1,),
        in_specs=[pl.BlockSpec((None, None, None, tokens, width), lambda j: (0, 0, 0, 0, 0))]
        + [pl.BlockSpec((4, part, HD), lambda j: (0, 0, 0))] * 4,
        out_specs=pl.BlockSpec((group, slots, rows, KVH * HD), lambda j: (0, 0, 0, 0)),
        scratch_shapes=[pltpu.VMEM((tokens, KVH * HD), BF),
                        pltpu.VMEM((width, KVH * HD), F32)],
        out_shape=jax.ShapeDtypeStruct((group, slots, rows, KVH * HD), BF),
        compiler_params=pltpu.CompilerParams(vmem_limit_bytes=16 << 20),
        cost_estimate=pl.CostEstimate(
            flops=2 * tokens * width * KVH * HD, bytes_accessed=3 << 20, transcendentals=0),
        name="first_grad",
    )(normed, *low)


def layer_grads(normed, low, high, rows):
    slots, tokens, width = normed.shape[2:]
    group = width // rows
    part = tokens // 4
    out_block = pl.BlockSpec((group, None, rows, KVH * HD), lambda j, *_: (0, j, 0, 0))
    return pl.pallas_call(
        functools.partial(grad_kernel, tokens, rows),
        grid_spec=pltpu.PrefetchScalarGridSpec(
            num_scalar_prefetch=0,
            grid=(slots,),
            in_specs=[pl.BlockSpec((None, None, None, tokens, width),
                                   lambda j, *_: (0, 0, j, 0, 0))]
            + [pl.BlockSpec((4, part, HD), lambda j, *_: (0, 0, 0))] * 8,
            out_specs=out_block,
            scratch_shapes=[pltpu.VMEM((tokens, KVH * HD), BF),
                            pltpu.VMEM((width, KVH * HD), F32)],
        ),
        out_shape=jax.ShapeDtypeStruct((group, slots, rows, KVH * HD), BF),
        compiler_params=pltpu.CompilerParams(vmem_limit_bytes=16 << 20),
        cost_estimate=pl.CostEstimate(
            flops=4 * tokens * width * KVH * HD, bytes_accessed=6 << 20, transcendentals=0),
        name="layer_grads",
    )(normed, *low, *high)


def adam_kernel(reps, sections, layers, batch, lmap, arrived, master, one, two,
                new_master, new_one, new_two, send):
    step = pl.program_id(0)

    @pl.when(step == 0)
    def _():
        send[...] = jnp.zeros_like(send)

    for i in range(batch):
        layer = step * batch + i
        total = None
        places = []
        for r in range(reps):
            section = lmap[r, layer]
            first, _ = first_and_count(lmap, r, section, layers)
            slot = layer - first
            source = r * sections + section
            places.append((source, slot))
            term = arrived[source, slot].astype(F32)
            total = term if total is None else total + term
        mean = total / reps
        m1 = BETA_ONE * one[i] + (1.0 - BETA_ONE) * mean
        m2 = BETA_TWO * two[i] + (1.0 - BETA_TWO) * mean * mean
        move = m1 / CORRECT_ONE / (jnp.sqrt(m2 / CORRECT_TWO) + EPSILON)
        updated = master[i] - LEARN_RATE * (move + DECAY_RATE * master[i])
        new_master[i] = updated
        new_one[i] = m1
        new_two[i] = m2
        rounded = updated.astype(BF)
        for source, slot in places:
            send[source, slot] = rounded


def adam(lmap, arrived, master, one, two):
    layers, _, rows, wide = master.shape
    reps = lmap.shape[0]
    batch = layers // 2
    state = pl.BlockSpec((batch, None, rows, wide), lambda l, *_: (l, 0, 0, 0))
    whole = pl.BlockSpec(arrived.shape, lambda l, *_: (0, 0, 0, 0))
    f32 = jax.ShapeDtypeStruct(master.shape, F32)
    return pl.pallas_call(
        functools.partial(adam_kernel, reps, arrived.shape[0] // reps, layers, batch),
        grid_spec=pltpu.PrefetchScalarGridSpec(
            num_scalar_prefetch=1,
            grid=(layers // batch,),
            in_specs=[whole, state, state, state],
            out_specs=[state, state, state, whole],
        ),
        out_shape=[f32, f32, f32, jax.ShapeDtypeStruct(arrived.shape, BF)],
        compiler_params=pltpu.CompilerParams(vmem_limit_bytes=16 << 20),
        cost_estimate=pl.CostEstimate(flops=20 * master.size, bytes_accessed=4 << 20,
                                      transcendentals=master.size),
        name="adamw",
    )(lmap, arrived, master, one, two)


def place_kernel(arrived, out, sem):
    copies = [pltpu.make_async_copy(arrived.at[:, j], out.at[j], sem.at[j])
              for j in range(out.shape[0])]
    for c in copies:
        c.start()
    for c in copies:
        c.wait()


def place(arrived):
    group, slots, rows, wide = arrived.shape
    return pl.pallas_call(
        place_kernel,
        in_specs=[pl.BlockSpec(memory_space=pl.ANY)],
        out_specs=pl.BlockSpec(memory_space=pl.ANY),
        scratch_shapes=[pltpu.SemaphoreType.DMA((slots,))],
        out_shape=jax.ShapeDtypeStruct((slots, group, rows, wide), BF),
        compiler_params=pltpu.CompilerParams(vmem_limit_bytes=4 << 20),
        cost_estimate=pl.CostEstimate(flops=0, bytes_accessed=2 << 20, transcendentals=0),
        name="place",
    )(arrived)


def shift(value, axis, by):
    n = lax.axis_size(axis)
    return lax.ppermute(value, axis, [(i, (i + by) % n) for i in range(n)])


def turn(value, by, along_x):
    pairs = []
    for core in range(2):
        for y in range(4):
            for x in range(4):
                if along_x == (core == 0):
                    to = (y, (x + by) % 4)
                else:
                    to = ((y + by) % 4, x)
                pairs.append(((core * 4 + y) * 4 + x, (core * 4 + to[0]) * 4 + to[1]))
    return lax.ppermute(value, ("core", "y", "x"), pairs)


def across(parts):
    total = parts[0].astype(F32)
    for k in (3, 1, 2):
        total = total + shift(parts[k], "x", k).astype(F32)
    return total.astype(BF)


def body(layer_section, token_count, window_size, normed_input, queries, key_rows, out_grad,
         master, moment_one, moment_two):
    layers = layer_section.shape[1]
    group_axes = ("rep", "z", "core")
    rows = master.shape[2]
    *parts, held = attention((layer_section, token_count, window_size),
                             queries, key_rows, out_grad, layers)

    def both_slots():
        block = across(parts)
        hops = {k: turn(block, k, True) for k in (3, 1, 2)}
        near = [block] + [hops[k] for k in range(1, 4)]
        low, high = jnp.stack([n[0] for n in near]), jnp.stack([n[1] for n in near])
        low_up, high_down = turn(low, 1, False), turn(high, 3, False)
        low_far, high_far = turn(low_up, 1, False), turn(high_down, 3, False)
        high_up, low_down = turn(high, 1, False), turn(low, 3, False)
        return layer_grads(normed_input, [low, low_up, low_far, low_down],
                           [high, high_up, high_far, high_down], rows)

    def one_slot():
        block = across([p[0] for p in parts])
        low = jnp.stack([block] + [turn(block, k, True) for k in range(1, 4)])
        low_up, low_down = turn(low, 1, False), turn(low, 3, False)
        return first_grad(normed_input, [low, low_up, turn(low_up, 1, False), low_down], rows)

    grads = lax.cond(held[0] == 2, both_slots, one_slot)
    arrived = lax.all_to_all(grads, group_axes, 0, 0, tiled=True)
    updated, first, second, send = adam(
        layer_section, arrived, master, moment_one, moment_two)
    weights = place(lax.all_to_all(send, group_axes, 0, 0, tiled=True))
    weights = weights.reshape(weights.shape[0], -1, weights.shape[3])
    return updated, first, second, weights[None, None]


def solution(mesh):
    reps, sections, tps = mesh.devices.shape
    fine = Mesh(mesh.devices.reshape(reps, 2, sections // 2, 4, tps // 4),
                ("rep", "z", "core", "y", "x"))
    section, tp = ("z", "core"), ("y", "x")
    wide = P("rep", section, None, None, tp)
    state = P(None, tp, ("rep",) + section, None)
    in_specs = (P(), P(), P(), wide, wide, P("rep", section, None, None, None), wide,
                state, state, state)
    out_specs = (state, state, state, P("rep", section, None, tp, None))
    return jax.shard_map(body, mesh=fine, in_specs=in_specs, out_specs=out_specs, check_vma=False)
```

```python
import functools

import jax
import jax.numpy as jnp
from jax import lax
from jax.experimental import pallas as pl
from jax.experimental.pallas import tpu as pltpu
from jax.sharding import Mesh, PartitionSpec as P

HQ = 32
KVH = 4
HD = 128
BETA_ONE = 0.9
BETA_TWO = 0.95
LEARN_RATE = 0.03
DECAY_RATE = 0.1
EPSILON = 1e-08
CORRECT_ONE = 0.9999734386011124
CORRECT_TWO = 0.994079470779667
LOG2E = 1.4426950408889634
TQ = 256
RB = 1536
VMEM = 60 << 20
BF = jnp.bfloat16
F32 = jnp.float32


def section_index():
    return 2 * lax.axis_index("z") + lax.axis_index("core")


def first_and_count(map_ref, replica, section, layers):
    first = jnp.int32(0)
    count = jnp.int32(0)
    for l in range(layers):
        at = map_ref[replica, l]
        first += (at < section).astype(jnp.int32)
        count += (at == section).astype(jnp.int32)
    return first, count


def attention_kernel(layers, tokens, per_dev, lmap, counts, windows,
                     q_ref, k_ref, g_ref, *rest):
    outs = rest[:4]
    flag, acc, p_scr, g_scr = rest[4:]
    slot, step = pl.program_id(0), pl.program_id(1)
    steps = pl.num_programs(1)
    replica, section, x_id = lax.axis_index("rep"), section_index(), lax.axis_index("x")
    first, held = first_and_count(lmap, replica, section, layers)
    flag[0] = held
    layer = jnp.minimum(first + slot, layers - 1)
    window = windows[layer]
    length = jnp.where(slot < held, counts[replica], 0)
    reach = tokens // 2 // TQ
    scale = HD ** (-0.5) * LOG2E

    @pl.when(step == 0)
    def _():
        acc[...] = jnp.zeros_like(acc)

    diff = (lax.broadcasted_iota(jnp.int32, (TQ, TQ), 1)
            - lax.broadcasted_iota(jnp.int32, (TQ, TQ), 0))

    def scores(sub, index, chunks, h):
        base = pl.multiple_of((index - (chunks - 1)) * TQ, TQ)
        query = q_ref[sub * TQ:(sub + 1) * TQ, h * HD:(h + 1) * HD]
        parts = []
        peak = None
        for c in range(chunks):
            s = lax.dot_general(
                k_ref[pl.ds(base + c * TQ, TQ), :], query, (((1,), (1,)), ((), ())),
                preferred_element_type=F32)
            off = (chunks - 1 - c) * TQ
            ok = None
            if c < 2:
                ok = diff < (window - off)
            if c == chunks - 1:
                ok = diff >= 0 if ok is None else ok & (diff >= 0)
            if ok is not None:
                s = jnp.where(ok, s, -1e30)
            parts.append(s)
            m = jnp.max(s, axis=0, keepdims=True)
            peak = m if peak is None else jnp.maximum(peak, m)
        return parts, peak

    def weigh(sub, index, h, parts, peak):
        shift = peak * scale
        total = None
        for c, s in enumerate(parts):
            e = jnp.exp2(s * scale - shift)
            t = jnp.sum(e, axis=0, keepdims=True)
            total = t if total is None else total + t
            p_scr[sub, c * TQ:(c + 1) * TQ, h * TQ:(h + 1) * TQ] = e.astype(BF)
        live = (index * TQ + lax.broadcasted_iota(jnp.int32, (1, TQ), 1)) < length
        inverse = jnp.where(live, 1.0 / total, 0.0)
        column = jnp.broadcast_to(inverse, (HD, TQ)).T
        grad = g_ref[sub * TQ:(sub + 1) * TQ, h * HD:(h + 1) * HD].astype(F32) * column
        g_scr[sub, h * TQ:(h + 1) * TQ, :] = grad.astype(BF)

    def spread(sub, index, chunks):
        base = pl.multiple_of((index - (chunks - 1)) * TQ, TQ)
        for c in range(chunks):
            acc[pl.ds(base + c * TQ, TQ), :] += jnp.dot(
                p_scr[sub, c * TQ:(c + 1) * TQ, :], g_scr[sub], preferred_element_type=F32)

    def run(counts):
        units = [(sub, h) for sub in range(len(counts)) for h in range(per_dev)]
        ready = {}
        late = []

        def score(u):
            if u < len(units):
                sub, h = units[u]
                ready[u] = scores(sub, len(counts) * step + sub, counts[sub], h)

        for u in range(2):
            score(u)
        for u, (sub, h) in enumerate(units):
            score(u + 2)
            for wait in [w for w in late if w[0] <= u]:
                spread(wait[1], len(counts) * step + wait[1], counts[wait[1]])
                late.remove(wait)
            weigh(sub, len(counts) * step + sub, h, *ready.pop(u))
            if h == per_dev - 1:
                late.append((u + 2, sub))
        for wait in late:
            spread(wait[1], len(counts) * step + wait[1], counts[wait[1]])

    deep = (window + TQ - 2) // TQ
    blocks = RB // TQ
    want = [jnp.minimum(blocks * step + i, deep) + 1 for i in range(blocks)]
    for counts in ((1, 2, 2, 2, 2, 2), (1, 2, 3, 3, 3, 3), (1, 2, 3, 4, 4, 4)):
        match = blocks * step * TQ < length
        for w, c in zip(want, counts):
            match = match & (w == c)

        @pl.when(match)
        def _(counts=counts):
            run(counts)

    @pl.when(step == steps - 1)
    def _():
        part = tokens // 4
        for k in range(4):
            at = pl.multiple_of(lax.rem(x_id + k, 4) * part, part)
            outs[k][...] = acc[pl.ds(at, part), :].astype(BF)


def attention(scalars, queries, key_rows, out_grad, layers):
    slots, tokens = queries.shape[2], queries.shape[3]
    per_dev = queries.shape[4] // HD
    part = tokens // 4
    wide = per_dev * HD
    row_block = pl.BlockSpec((None, None, None, RB, wide), lambda j, i, *_: (0, 0, j, i, 0))
    key_block = pl.BlockSpec(
        (None, None, None, tokens, HD), lambda j, i, *_: (0, 0, j, 0, lax.axis_index("y")))
    out_block = pl.BlockSpec((None, part, HD), lambda j, i, *_: (j, 0, 0))
    return pl.pallas_call(
        functools.partial(attention_kernel, layers, tokens, per_dev),
        grid_spec=pltpu.PrefetchScalarGridSpec(
            num_scalar_prefetch=3,
            grid=(slots, tokens // RB),
            in_specs=[row_block, key_block, row_block],
            out_specs=[out_block] * 4 + [pl.BlockSpec(memory_space=pltpu.SMEM)],
            scratch_shapes=[
                pltpu.VMEM((tokens, HD), F32),
                pltpu.VMEM((6, tokens // 2 + TQ, per_dev * TQ), BF),
                pltpu.VMEM((6, per_dev * TQ, HD), BF),
            ],
        ),
        out_shape=[jax.ShapeDtypeStruct((slots, part, HD), BF)] * 4
        + [jax.ShapeDtypeStruct((1,), jnp.int32)],
        compiler_params=pltpu.CompilerParams(vmem_limit_bytes=VMEM),
        cost_estimate=pl.CostEstimate(
            flops=36 * per_dev * 4 * TQ * TQ * HD, bytes_accessed=4 << 20,
            transcendentals=36 * per_dev * TQ * TQ),
        name="attention",
    )(*scalars, queries, key_rows, out_grad)


def grad_slot(tokens, rows, x_ref, pieces, out_ref, value, result):
    core, y_id, x_id = (lax.axis_index(n) for n in ("core", "y", "x"))
    part = tokens // 4
    for k in range(4):
        for i in range(4):
            y = lax.rem(y_id + 4 - jnp.where(core == 0, k, i), 4)
            x = lax.rem(x_id + 4 - jnp.where(core == 0, i, k), 4)
            at = pl.multiple_of(x * part, part)
            col = pl.multiple_of(y * HD, HD)
            value[pl.ds(at, part), pl.ds(col, HD)] = pieces[k][i]
    result[...] = lax.dot_general(
        x_ref[...], value[...], (((0,), (0,)), ((), ())), preferred_element_type=F32)
    for z in range(out_ref.shape[0]):
        out_ref[z] = result[z * rows:(z + 1) * rows, :].astype(BF)


def grad_kernel(tokens, rows, x_ref, *refs):
    for slot in range(2):
        @pl.when(pl.program_id(0) == slot)
        def _(pieces=refs[4 * slot:4 * slot + 4], slot=slot):
            grad_slot(tokens, rows, x_ref, pieces, refs[8].at[:, slot], *refs[9:])


def first_kernel(tokens, rows, x_ref, *refs):
    out_ref = refs[4]
    grad_slot(tokens, rows, x_ref, refs[:4], out_ref.at[:, 0], *refs[5:])
    out_ref[:, 1] = jnp.zeros(out_ref.shape[:1] + out_ref.shape[2:], BF)


def first_grad(normed, low, rows):
    slots, tokens, width = normed.shape[2:]
    group = width // rows
    part = tokens // 4
    return pl.pallas_call(
        functools.partial(first_kernel, tokens, rows),
        grid=(1,),
        in_specs=[pl.BlockSpec((None, None, None, tokens, width), lambda j: (0, 0, 0, 0, 0))]
        + [pl.BlockSpec((4, part, HD), lambda j: (0, 0, 0))] * 4,
        out_specs=pl.BlockSpec((group, slots, rows, KVH * HD), lambda j: (0, 0, 0, 0)),
        scratch_shapes=[pltpu.VMEM((tokens, KVH * HD), BF),
                        pltpu.VMEM((width, KVH * HD), F32)],
        out_shape=jax.ShapeDtypeStruct((group, slots, rows, KVH * HD), BF),
        compiler_params=pltpu.CompilerParams(vmem_limit_bytes=16 << 20),
        cost_estimate=pl.CostEstimate(
            flops=2 * tokens * width * KVH * HD, bytes_accessed=3 << 20, transcendentals=0),
        name="first_grad",
    )(normed, *low)


def layer_grads(normed, low, high, rows):
    slots, tokens, width = normed.shape[2:]
    group = width // rows
    part = tokens // 4
    out_block = pl.BlockSpec(memory_space=pltpu.VMEM)
    return pl.pallas_call(
        functools.partial(grad_kernel, tokens, rows),
        grid_spec=pltpu.PrefetchScalarGridSpec(
            num_scalar_prefetch=0,
            grid=(slots,),
            in_specs=[pl.BlockSpec((None, None, None, tokens, width),
                                   lambda j, *_: (0, 0, j, 0, 0))]
            + [pl.BlockSpec((4, part, HD), lambda j, *_: (0, 0, 0))] * 8,
            out_specs=out_block,
            scratch_shapes=[pltpu.VMEM((tokens, KVH * HD), BF),
                            pltpu.VMEM((width, KVH * HD), F32)],
        ),
        out_shape=jax.ShapeDtypeStruct((group, slots, rows, KVH * HD), BF),
        compiler_params=pltpu.CompilerParams(vmem_limit_bytes=16 << 20),
        cost_estimate=pl.CostEstimate(
            flops=4 * tokens * width * KVH * HD, bytes_accessed=6 << 20, transcendentals=0),
        name="layer_grads",
    )(normed, *low, *high)


def adam_kernel(reps, sections, layers, batch, lmap, arrived, master, one, two,
                new_master, new_one, new_two, send):
    step = pl.program_id(0)

    @pl.when(step == 0)
    def _():
        send[...] = jnp.zeros_like(send)

    for i in range(batch):
        layer = i
        total = None
        places = []
        for r in range(reps):
            section = lmap[r, layer]
            slot = (lmap[r, layer - 1] == section).astype(jnp.int32) if layer else 0
            source = r * sections + section
            places.append((source, slot))
            term = arrived[source, slot].astype(F32)
            total = term if total is None else total + term
        mean = total / reps
        m1 = BETA_ONE * one[i] + (1.0 - BETA_ONE) * mean
        m2 = BETA_TWO * two[i] + (1.0 - BETA_TWO) * mean * mean
        move = m1 / CORRECT_ONE / (jnp.sqrt(m2 / CORRECT_TWO) + EPSILON)
        updated = master[i] - LEARN_RATE * (move + DECAY_RATE * master[i])
        new_master[i] = updated
        new_one[i] = m1
        new_two[i] = m2
        rounded = updated.astype(BF)
        for source, slot in places:
            send[source, slot] = rounded


def adam(lmap, arrived, master, one, two):
    layers, _, rows, wide = master.shape
    reps = lmap.shape[0]
    batch = layers
    state = pl.BlockSpec((batch, None, rows, wide), lambda l, *_: (l, 0, 0, 0))
    resident = pl.BlockSpec(memory_space=pltpu.VMEM)
    f32 = jax.ShapeDtypeStruct(master.shape, F32)
    return pl.pallas_call(
        functools.partial(adam_kernel, reps, arrived.shape[0] // reps, layers, batch),
        grid_spec=pltpu.PrefetchScalarGridSpec(
            num_scalar_prefetch=1,
            grid=(layers // batch,),
            in_specs=[resident, state, state, state],
            out_specs=[state, state, state, resident],
        ),
        out_shape=[f32, f32, f32, jax.ShapeDtypeStruct(arrived.shape, BF)],
        compiler_params=pltpu.CompilerParams(vmem_limit_bytes=16 << 20),
        cost_estimate=pl.CostEstimate(flops=20 * master.size, bytes_accessed=4 << 20,
                                      transcendentals=master.size),
        name="adamw",
    )(lmap, arrived, master, one, two)


def place_kernel(arrived, out, sem):
    copies = [pltpu.make_async_copy(arrived.at[:, j], out.at[j], sem.at[j])
              for j in range(out.shape[0])]
    for c in copies:
        c.start()
    for c in copies:
        c.wait()


def place(arrived):
    group, slots, rows, wide = arrived.shape
    return pl.pallas_call(
        place_kernel,
        in_specs=[pl.BlockSpec(memory_space=pl.ANY)],
        out_specs=pl.BlockSpec(memory_space=pl.ANY),
        scratch_shapes=[pltpu.SemaphoreType.DMA((slots,))],
        out_shape=jax.ShapeDtypeStruct((slots, group, rows, wide), BF),
        compiler_params=pltpu.CompilerParams(vmem_limit_bytes=4 << 20),
        cost_estimate=pl.CostEstimate(flops=0, bytes_accessed=2 << 20, transcendentals=0),
        name="place",
    )(arrived)


def shift(value, axis, by):
    n = lax.axis_size(axis)
    return lax.ppermute(value, axis, [(i, (i + by) % n) for i in range(n)])


def turn(value, by, along_x):
    pairs = []
    for core in range(2):
        for y in range(4):
            for x in range(4):
                if along_x == (core == 0):
                    to = (y, (x + by) % 4)
                else:
                    to = ((y + by) % 4, x)
                pairs.append(((core * 4 + y) * 4 + x, (core * 4 + to[0]) * 4 + to[1]))
    return lax.ppermute(value, ("core", "y", "x"), pairs)


def across(parts):
    total = parts[0].astype(F32)
    for k in (3, 1, 2):
        total = total + shift(parts[k], "x", k).astype(F32)
    return total.astype(BF)


def body(layer_section, token_count, window_size, normed_input, queries, key_rows, out_grad,
         master, moment_one, moment_two):
    layers = layer_section.shape[1]
    group_axes = ("rep", "z", "core")
    rows = master.shape[2]
    *parts, held = attention((layer_section, token_count, window_size),
                             queries, key_rows, out_grad, layers)

    def both_slots():
        block = across(parts)
        hops = {k: turn(block, k, True) for k in (3, 1, 2)}
        near = [block] + [hops[k] for k in range(1, 4)]
        low, high = jnp.stack([n[0] for n in near]), jnp.stack([n[1] for n in near])
        low_up, high_down = turn(low, 1, False), turn(high, 3, False)
        low_far, high_far = turn(low_up, 1, False), turn(high_down, 3, False)
        high_up, low_down = turn(high, 1, False), turn(low, 3, False)
        return layer_grads(normed_input, [low, low_up, low_far, low_down],
                           [high, high_up, high_far, high_down], rows)

    def one_slot():
        block = across([p[0] for p in parts])
        low = jnp.stack([block] + [turn(block, k, True) for k in range(1, 4)])
        low_up, low_down = turn(low, 1, False), turn(low, 3, False)
        return first_grad(normed_input, [low, low_up, turn(low_up, 1, False), low_down], rows)

    grads = lax.cond(held[0] == 2, both_slots, one_slot)
    arrived = lax.all_to_all(grads, group_axes, 0, 0, tiled=True)
    updated, first, second, send = adam(
        layer_section, arrived, master, moment_one, moment_two)
    weights = place(lax.all_to_all(send, group_axes, 0, 0, tiled=True))
    weights = weights.reshape(weights.shape[0], -1, weights.shape[3])
    return updated, first, second, weights[None, None]


def solution(mesh):
    reps, sections, tps = mesh.devices.shape
    fine = Mesh(mesh.devices.reshape(reps, 2, sections // 2, 4, tps // 4),
                ("rep", "z", "core", "y", "x"))
    section, tp = ("z", "core"), ("y", "x")
    wide = P("rep", section, None, None, tp)
    state = P(None, tp, ("rep",) + section, None)
    in_specs = (P(), P(), P(), wide, wide, P("rep", section, None, None, None), wide,
                state, state, state)
    out_specs = (state, state, state, P("rep", section, None, tp, None))
    return jax.shard_map(body, mesh=fine, in_specs=in_specs, out_specs=out_specs, check_vma=False)
```
